512 devices in a mesh: seq: 16 (over y, z_lo), fsdp: 32 (over z_hi, x, core).
Axes of the slice: x: 4, y: 8, z: 8 (z_hi: 4, z_lo: 2; z = z_hi * 2 + z_lo), core: 2. Of those that a mesh axis runs over, the one named last changes fastest.
Arguments:
- q_video: bfloat16 [32, 1920, 1536], P('fsdp', 'seq'), may hold values from -42 to 42
- kv_video: bfloat16 [32, 1920, 2, 1536], P('fsdp', 'seq'), may hold values from -6 to 6
- q_text: bfloat16 [32, 128, 1536], P('fsdp', 'seq'), may hold values from -6 to 6
- kv_text: bfloat16 [32, 128, 2, 1536], P('fsdp', 'seq'), may hold values from -9 to 9
- text_lengths: int32 [32], P('fsdp'), may hold values from 1 to 128, as said below
- gate: float32 [32, 1536], P('fsdp'), may hold values from 0.5 to 4
- w_out: bfloat16 [1536, 1536], P('fsdp'), may hold values from -0.15625 to 0.15625
Outputs:
- attn_video: bfloat16 [32, 1920, 1536], P('fsdp', 'seq')
- attn_text: bfloat16 [32, 128, 1536], P('fsdp', 'seq')
- lse_video: float32 [32, 12, 1920], P('fsdp', None, 'seq')
- lse_text: float32 [32, 12, 128], P('fsdp', None, 'seq')
- proj_video: bfloat16 [32, 1920, 1536], P('fsdp', 'seq')
The draws below stay inside these ranges and needn't reach their ends.
Inputs may be any that keep to these rules, and one draw needn't show every extreme that they name: `text_lengths`: some sample has all 128 text slots real.
All inputs are finite; a program needn't handle non-finite values.
Results may differ from the reference program's by a relative error of at most 0.018.
Values may be sent and summed in bfloat16 or wider, within the bound.
No kernel may reach another device: no remote copies, remote signals or barrier semaphores. Data moves between devices by JAX's collectives and lax.ppermute only.
A program may use at most 128 MiB of HBM per device.

```python
import math
import jax
import jax.numpy as jnp
from jax import lax

HEADS = 12
HEAD = 128
DOUT = 1536
HD = 1536
VID = 1920
TXT = 128
BATCH = 32


def common_field(key):
    shape = (BATCH, VID, HD)
    second = jax.random.fold_in(key, 1)
    bell = jnp.clip(jax.random.normal(second, shape, jnp.float32), -6.0, 6.0)
    return bell


def draw_q_video(key, part):
    shape = (BATCH, VID, HD)
    key = jax.random.fold_in(key, 13)
    queries = jnp.clip(2.2 * jax.random.normal(key, shape, jnp.float32), -13.0, 13.0)
    return queries.astype(jnp.bfloat16)


def draw_kv_video(key, part):
    shape = (BATCH, VID, HD)
    shared = common_field(key)
    key = jax.random.fold_in(key, 11)
    keys = shared
    values = jnp.clip(jax.random.normal(key, shape, jnp.float32), -6.0, 6.0)
    return jnp.stack([keys, values], axis=2).astype(jnp.bfloat16)


def draw_text_lengths(key, part):
    key = jax.random.fold_in(key, 7)
    first, second = jax.random.split(key)
    counts = jax.random.randint(first, (BATCH,), 1, TXT + 1)
    chosen = jax.random.randint(second, (), 0, BATCH)
    return jnp.where(jnp.arange(BATCH) == chosen, TXT, counts).astype(jnp.int32)


def steps_of(stream_key, dims, shards, least, high):
    factor_of, own = 1.0, jax.random.fold_in(stream_key, 6)
    for dim, shards_of in shards:
        heights = jnp.exp(jax.random.uniform(jax.random.fold_in(own, dim), (shards_of,), jnp.float32, least / len(shards), high / len(shards)))
        factor_of = factor_of * jnp.repeat(heights, dims[dim] // shards_of).reshape([-1 if axis == dim else 1 for axis in range(len(dims))])
    return factor_of


def scatter_about(stream_key, dims, spread, limit, cuts=(), held_as=jnp.bfloat16):
    entries = jax.random.normal(stream_key, dims, jnp.float32) * spread
    if len(cuts) > 0:
        entries = steps_of(stream_key, dims, cuts, -0.22, 0.18) * entries
    return jnp.clip(entries, min=-limit, max=limit).astype(held_as)


def setup_inputs(seed: int = 0) -> dict:
    arg_keys = jax.random.split(jax.random.key(seed), 8)
    return {
        "q_video": draw_q_video(jax.random.fold_in(arg_keys[7], 71), 0),
        "kv_video": draw_kv_video(jax.random.fold_in(arg_keys[7], 71), 0),
        "q_text": scatter_about(arg_keys[2], (BATCH, TXT, HD), 1.0, 6.0, ((0, 32), (1, 16))),
        "kv_text": scatter_about(arg_keys[3], (BATCH, TXT, 2, HD), 1.5, 9.0, ((0, 32), (1, 16))),
        "text_lengths": draw_text_lengths(jax.random.fold_in(arg_keys[7], 71), 0),
        "gate": jnp.clip(jnp.exp(math.log(4.0) - 2.0794415 * jax.random.uniform(arg_keys[5], (BATCH, DOUT), jnp.float32) ** steps_of(arg_keys[5], (BATCH, DOUT), ((0, 32),), -0.2, 0.2)), 0.5, 4.0),
        "w_out": scatter_about(arg_keys[6], (HD, DOUT), HD ** -0.5, 0.15625, ((0, 32),)),
    }


def reference(q_video, kv_video, q_text, kv_text, text_lengths, gate, w_out):

    def one_sample(item):
        q_vid, kv_vid, q_txt, kv_txt, length, gain = item
        queries = jnp.concatenate([q_vid, q_txt], 0).astype(jnp.float32).reshape(-1, HEADS, HEAD)
        keyvals = jnp.concatenate([kv_vid, kv_txt], 0).astype(jnp.float32)
        keys = keyvals[:, 0].reshape(-1, HEADS, HEAD)
        values = keyvals[:, 1].reshape(-1, HEADS, HEAD)
        valid = jnp.concatenate([jnp.ones((VID,), bool), jnp.arange(TXT) < length])
        scores = jnp.einsum('qhd,khd->hqk', queries, keys) * (1.0 / math.sqrt(HEAD))
        scores = jnp.where(valid[None, None, :], scores, -1e+30)
        top = lax.optimization_barrier(jnp.max(scores, axis=-1, keepdims=True))
        lse = top[..., 0] + jnp.log(lax.optimization_barrier(jnp.sum(jnp.exp(scores - top), axis=-1)))
        probs = jnp.exp(scores - lse[..., None]).astype(jnp.bfloat16)
        mixed = jnp.einsum('hqk,khd->qhd', probs.astype(jnp.float32), values)
        mixed = mixed.reshape(-1, HD).astype(jnp.bfloat16)
        video_rows = mixed[:VID]
        projected = jnp.dot(video_rows, w_out, preferred_element_type=jnp.float32)
        projected = (projected * gain[None, :]).astype(jnp.bfloat16)
        return (video_rows, mixed[VID:], lse[:, :VID], lse[:, VID:], projected)
    return tuple(lax.map(one_sample, (q_video, kv_video, q_text, kv_text, text_lengths, gate)))
```

```python
import functools
import math

import jax
import jax.numpy as jnp
from jax import lax
from jax.experimental import pallas as pl
from jax.experimental.pallas import tpu as pltpu
from jax.sharding import PartitionSpec as P

HEADS = 12
HEAD = 128
SLOPE = math.log2(math.e) / math.sqrt(HEAD)
LN2 = math.log(2.0)
LSE_ROWS = 16
VMEM = pltpu.VMEM


def pack_kernel(length_ref, base_ref, qv_ref, kvv_ref, qt_ref, kvt_ref, out_ref):
    vid = qv_ref.shape[0]
    txt = qt_ref.shape[0]
    slot = base_ref[0] + lax.broadcasted_iota(jnp.int32, (txt, HEAD), 0)
    valid = slot < length_ref[0]
    for h in range(HEADS):
        cols = pl.ds(h * HEAD, HEAD)
        out_ref[h, 0, :vid] = qv_ref[:, cols]
        out_ref[h, 0, vid:] = qt_ref[:, cols]
        keys = kvv_ref[:, cols]
        out_ref[h, 1, :vid] = keys
        out_ref[h, 1, vid:] = jnp.where(
            valid, kvt_ref[:, cols].astype(jnp.float32), keys[:1].astype(jnp.float32)
        ).astype(jnp.bfloat16)
        vcols = pl.ds((HEADS + h) * HEAD, HEAD)
        out_ref[h, 2, :vid] = kvv_ref[:, vcols]
        out_ref[h, 2, vid:] = jnp.where(
            valid, kvt_ref[:, vcols].astype(jnp.float32), 0.0
        ).astype(jnp.bfloat16)
    for h in range(HEADS, out_ref.shape[0]):
        out_ref[h] = jnp.zeros(out_ref.shape[1:], jnp.bfloat16)


def attend_kernel(vid, length_ref, x_ref, out_ref, vals_ref, keys_ref):
    sources, _, rows, _ = x_ref.shape
    txt = rows - vid
    step = pl.program_id(0)
    per = out_ref.shape[0]

    @pl.when(step == 0)
    def _():
        row = lax.broadcasted_iota(jnp.int32, (rows, HEAD), 0)
        for s in range(sources):
            valid = (row < vid) | (row - vid + s * txt < length_ref[0])
            keys_ref[pl.ds(s * rows, rows), :] = x_ref[s, 1]
            vals_ref[pl.ds(s * rows, rows), :HEAD] = x_ref[s, 2]
            vals_ref[pl.ds(s * rows, rows), HEAD:] = jnp.where(valid, 1.0, 0.0).astype(jnp.bfloat16)

    for j in range(per):
        q = x_ref[step * per + j, 0]
        scores = lax.dot_general(
            q, keys_ref[...], (((1,), (1,)), ((), ())), preferred_element_type=jnp.float32
        )
        best = jnp.max(scores, axis=1, keepdims=True) * SLOPE
        weights = jnp.exp2(scores * SLOPE - best).astype(jnp.bfloat16)
        both = jnp.dot(weights, vals_ref[...], preferred_element_type=jnp.float32)
        total = both[:, HEAD:]
        out_ref[j, :rows] = (both[:, :HEAD] / total).astype(jnp.bfloat16)
        lse = ((best + jnp.log2(total)) * LN2).T[:LSE_ROWS]
        high = lse.astype(jnp.bfloat16).astype(jnp.float32)
        mid = (lse - high).astype(jnp.bfloat16).astype(jnp.float32)
        low = lse - high - mid
        which = lax.broadcasted_iota(jnp.int32, lse.shape, 0)
        parts = jnp.where(which == 0, high, jnp.where(which == 1, mid, low))
        out_ref[j, rows:] = parts.astype(jnp.bfloat16)


def project_kernel(x_ref, w_ref, gate_ref, av_ref, at_ref, lv_ref, lt_ref, pv_ref):
    vid = av_ref.shape[0]
    rows = vid + at_ref.shape[0]
    mixed = jnp.concatenate([x_ref[h, :rows] for h in range(HEADS)], axis=1)

    @pl.when(pl.program_id(0) == 0)
    def _():
        av_ref[...] = mixed[:vid]
        at_ref[...] = mixed[vid:]
        for h in range(HEADS):
            parts = x_ref[h, rows:].astype(jnp.float32)
            lse = parts[0:1] + parts[1:2] + parts[2:3]
            lv_ref[pl.ds(h, 1), :] = lse[:, :vid]
            lt_ref[pl.ds(h, 1), :] = lse[:, vid:]

    out = jnp.dot(mixed, w_ref[...], preferred_element_type=jnp.float32)
    pv_ref[...] = (out[:vid] * gate_ref[...]).astype(jnp.bfloat16)


def shards(sources, q_video, kv_video, q_text, kv_text, text_lengths, gate, w_out):
    vid, feats = q_video.shape[1:]
    txt = q_text.shape[1]
    rows = vid + txt
    base = (lax.axis_index("seq") * txt).astype(jnp.int32).reshape(1)
    whole_w = lax.all_gather(w_out, "fsdp", axis=0, tiled=True)
    smem = pl.BlockSpec(memory_space=pltpu.SMEM)
    vmem = pl.BlockSpec(memory_space=VMEM)
    packed = pl.pallas_call(
        pack_kernel,
        out_shape=jax.ShapeDtypeStruct((sources, 3, rows, HEAD), jnp.bfloat16),
        in_specs=[smem, smem, vmem, vmem, vmem, vmem],
        out_specs=vmem,
        name="pack",
    )(
        text_lengths,
        base,
        q_video[0],
        kv_video.reshape(vid, 2 * feats),
        q_text[0],
        kv_text.reshape(txt, 2 * feats),
    )
    moved = lax.all_to_all(packed, "seq", 0, 0, tiled=True)
    per = 2
    mixed = pl.pallas_call(
        functools.partial(attend_kernel, vid),
        grid=(sources // per,),
        out_shape=jax.ShapeDtypeStruct((sources, rows + LSE_ROWS, HEAD), jnp.bfloat16),
        in_specs=[smem, vmem],
        out_specs=pl.BlockSpec((per, rows + LSE_ROWS, HEAD), lambda i: (i, 0, 0)),
        scratch_shapes=[
            VMEM((sources * rows, 2 * HEAD), jnp.bfloat16),
            VMEM((sources * rows, HEAD), jnp.bfloat16),
        ],
        compiler_params=pltpu.CompilerParams(vmem_limit_bytes=32 << 20),
        name="attend",
    )(text_lengths, moved)
    back = lax.all_to_all(mixed, "seq", 0, 0, tiled=True)
    cols = 512
    outs = pl.pallas_call(
        project_kernel,
        grid=(feats // cols,),
        out_shape=(
            jax.ShapeDtypeStruct((vid, feats), jnp.bfloat16),
            jax.ShapeDtypeStruct((txt, feats), jnp.bfloat16),
            jax.ShapeDtypeStruct((HEADS, vid), jnp.float32),
            jax.ShapeDtypeStruct((HEADS, txt), jnp.float32),
            jax.ShapeDtypeStruct((vid, feats), jnp.bfloat16),
        ),
        in_specs=[
            vmem,
            pl.BlockSpec((feats, cols), lambda i: (0, i)),
            pl.BlockSpec((1, cols), lambda i: (0, i)),
        ],
        out_specs=(vmem, vmem, vmem, vmem, pl.BlockSpec((vid, cols), lambda i: (0, i))),
        compiler_params=pltpu.CompilerParams(vmem_limit_bytes=32 << 20),
        name="project",
    )(back, whole_w, gate)
    return tuple(out[None] for out in outs)


def solution(mesh):
    placed = (
        P("fsdp", "seq", None),
        P("fsdp", "seq", None, None),
        P("fsdp", "seq", None),
        P("fsdp", "seq", None, None),
        P("fsdp"),
        P("fsdp", None),
        P("fsdp", None),
    )
    return jax.shard_map(
        functools.partial(shards, mesh.shape["seq"]),
        mesh=mesh,
        in_specs=placed,
        out_specs=(
            P("fsdp", "seq", None),
            P("fsdp", "seq", None),
            P("fsdp", None, "seq"),
            P("fsdp", None, "seq"),
            P("fsdp", "seq", None),
        ),
        check_vma=False,
    )
```

```python
import functools
import math

import jax
import jax.numpy as jnp
from jax import lax
from jax.experimental import pallas as pl
from jax.experimental.pallas import tpu as pltpu
from jax.sharding import Mesh
from jax.sharding import PartitionSpec as P

HEADS = 12
HEAD = 128
SLOPE = math.log2(math.e) / math.sqrt(HEAD)
LN2 = math.log(2.0)
LSE_ROWS = 16
FSDP = (4, 4, 2)
FSDP_AXES = ("zh", "x", "core")
GROUP = 4
VMEM = pltpu.VMEM


def pack_kernel(
    length_ref, base_ref, qv_hbm, kvv_hbm, qt_hbm, kvt_hbm, out_ref,
    qv_ref, kvv_ref, qt_ref, kvt_ref, split_ref, sems,
):
    vid = qv_ref.shape[0]
    txt = qt_ref.shape[0]
    pairs = ((kvv_hbm, kvv_ref), (kvt_hbm, kvt_ref), (qv_hbm, qv_ref), (qt_hbm, qt_ref))
    copies = [pltpu.make_async_copy(a, b, sems.at[i]) for i, (a, b) in enumerate(pairs)]
    for copy in copies:
        copy.start()
    for h in range(HEADS, out_ref.shape[0]):
        out_ref[h] = jnp.zeros(out_ref.shape[1:], jnp.bfloat16)
    copies[0].wait()
    copies[1].wait()
    slot = base_ref[0] + lax.broadcasted_iota(jnp.int32, (txt, HEAD), 0)
    valid = slot < length_ref[0]
    for h in range(HEADS):
        cols = pl.ds(h * HEAD, HEAD)
        video = kvv_ref[:, :, cols].astype(jnp.float32).reshape(2 * vid, HEAD)
        text = kvt_ref[:, :, cols].astype(jnp.float32).reshape(2 * txt, HEAD)
        split_ref[h, : 2 * vid] = video
        split_ref[h, 2 * vid :] = text
        keys = split_ref[h, pl.ds(0, vid, stride=2), :]
        text_keys = split_ref[h, pl.ds(2 * vid, txt, stride=2), :]
        text_values = split_ref[h, pl.ds(2 * vid + 1, txt, stride=2), :]
        out_ref[h, 1, :vid] = keys.astype(jnp.bfloat16)
        out_ref[h, 1, vid:] = jnp.where(valid, text_keys, keys[:1]).astype(jnp.bfloat16)
        out_ref[h, 2, :vid] = split_ref[h, pl.ds(1, vid, stride=2), :].astype(jnp.bfloat16)
        out_ref[h, 2, vid:] = jnp.where(valid, text_values, 0.0).astype(jnp.bfloat16)
    copies[2].wait()
    copies[3].wait()
    for h in range(HEADS):
        cols = pl.ds(h * HEAD, HEAD)
        out_ref[h, 0, :vid] = qv_ref[:, cols]
        out_ref[h, 0, vid:] = qt_ref[:, cols]


def attend_kernel(vid, length_ref, x_ref, out_ref, vals_ref, keys_ref, queries_ref):
    sources, _, rows, _ = x_ref.shape
    txt = rows - vid
    row = lax.broadcasted_iota(jnp.int32, (rows, HEAD), 0)
    for s in range(sources):
        valid = (row < vid) | (row - vid + s * txt < length_ref[0])
        here = pl.ds(s * rows, rows)
        queries_ref[here, :] = x_ref[s, 0]
        keys_ref[here, :] = x_ref[s, 1]
        vals_ref[here, :HEAD] = x_ref[s, 2]
        vals_ref[here, HEAD:] = jnp.where(valid, 1.0, 0.0).astype(jnp.bfloat16)

    def score(block):
        return lax.dot_general(
            queries_ref[pl.ds(block * GROUP * rows, GROUP * rows), :],
            keys_ref[...],
            (((1,), (1,)), ((), ())),
            preferred_element_type=jnp.float32,
        )

    blocks = sources // GROUP
    following = score(0)
    for block in range(blocks):
        scores = following
        if block + 1 < blocks:
            following = score(block + 1)
        best = jnp.max(scores, axis=1, keepdims=True) * SLOPE
        weights = jnp.exp2(scores * SLOPE - best).astype(jnp.bfloat16)
        both = jnp.dot(weights, vals_ref[...], preferred_element_type=jnp.float32)
        total = both[:, HEAD:]
        mixed = (both[:, :HEAD] / total).astype(jnp.bfloat16)
        wide = (best + jnp.log2(total)) * LN2
        for g in range(GROUP):
            s = block * GROUP + g
            out_ref[s, :rows] = mixed[g * rows : (g + 1) * rows]
            lse = wide[g * rows : (g + 1) * rows].T[:LSE_ROWS]
            high = lse.astype(jnp.bfloat16).astype(jnp.float32)
            mid = (lse - high).astype(jnp.bfloat16).astype(jnp.float32)
            which = lax.broadcasted_iota(jnp.int32, lse.shape, 0)
            parts = jnp.where(which == 0, high, jnp.where(which == 1, mid, lse - high - mid))
            out_ref[s, rows:] = parts.astype(jnp.bfloat16)


def project_kernel(place, *refs):
    x_ref, gate_ref, spot_ref, *pieces = refs[: -7]
    av_ref, at_ref, lv_ref, lt_ref, pv_ref, w_ref, sem = refs[-7:]
    vid = av_ref.shape[0]
    rows = vid + at_ref.shape[0]
    copies = [
        pltpu.make_async_copy(
            pieces[i].at[pl.ds(first, count), :],
            w_ref.at[pl.ds(pl.multiple_of(target, 16), count), :],
            sem,
        )
        for i, first, target, count in place(spot_ref)
    ]
    for copy in copies:
        copy.start()
    lses = []
    for h in range(HEADS):
        cols = pl.ds(h * HEAD, HEAD)
        av_ref[:, cols] = x_ref[h, :vid]
        at_ref[:, cols] = x_ref[h, vid:rows]
        parts = x_ref[h, rows:].astype(jnp.float32)
        lse = parts[0:1] + parts[1:2] + parts[2:3]
        lv_ref[h] = lse[:, :vid]
        lses.append(lse)
    lses += [lses[0]] * (HEAD - HEADS)
    lt_ref[...] = jnp.concatenate(lses, axis=0).T[vid:, :HEADS]
    for copy in copies:
        copy.wait()
    out = jnp.dot(av_ref[...], w_ref[...], preferred_element_type=jnp.float32)
    pv_ref[...] = (out * gate_ref[...]).astype(jnp.bfloat16)


def spot_of(zh, x, core, count):
    return ((zh * FSDP[1] + x) * FSDP[2] + core) * count


def ring(block, axis):
    n = lax.axis_size(axis)
    return [block] + [
        lax.ppermute(block, axis, [(i, (i + s) % n) for i in range(n)]) for s in range(1, n)
    ]


def gathered(w_out):
    column = jnp.concatenate(ring(w_out, "zh"), axis=0)
    mine = ring(column, "x")
    return (*mine, *(lax.ppermute(part, "core", [(0, 1), (1, 0)]) for part in mine))


def place(count, spot_ref):
    zh, x, core = spot_ref[0], spot_ref[1], spot_ref[2]
    return [
        (
            other * FSDP[1] + dx,
            dz * count,
            spot_of((zh + FSDP[0] - dz) % FSDP[0], (x + FSDP[1] - dx) % FSDP[1], core ^ other, count),
            count,
        )
        for other in range(FSDP[2])
        for dx in range(FSDP[1])
        for dz in range(FSDP[0])
    ]


def shards(sources, q_video, kv_video, q_text, kv_text, text_lengths, gate, w_out):
    vid, feats = q_video.shape[1:]
    txt = q_text.shape[1]
    rows = vid + txt
    base = (lax.axis_index("seq") * txt).astype(jnp.int32).reshape(1)
    pieces = gathered(w_out)
    spot = jnp.stack([lax.axis_index(axis) for axis in ("zh", "x", "core")]).astype(jnp.int32)
    smem = pl.BlockSpec(memory_space=pltpu.SMEM)
    vmem = pl.BlockSpec(memory_space=VMEM)
    anywhere = pl.BlockSpec(memory_space=pl.ANY)
    packed = pl.pallas_call(
        pack_kernel,
        out_shape=jax.ShapeDtypeStruct((sources, 3, rows, HEAD), jnp.bfloat16),
        in_specs=[smem, smem, anywhere, anywhere, anywhere, anywhere],
        out_specs=vmem,
        scratch_shapes=[
            VMEM((vid, feats), jnp.bfloat16),
            VMEM((vid, 2, feats), jnp.bfloat16),
            VMEM((txt, feats), jnp.bfloat16),
            VMEM((txt, 2, feats), jnp.bfloat16),
            VMEM((HEADS, 2 * rows, HEAD), jnp.float32),
            pltpu.SemaphoreType.DMA((4,)),
        ],
        compiler_params=pltpu.CompilerParams(vmem_limit_bytes=60 << 20),
        name="pack",
    )(
        text_lengths,
        base,
        q_video[0],
        kv_video[0],
        q_text[0],
        kv_text[0],
    )
    moved = lax.all_to_all(packed, "seq", 0, 0, tiled=True)
    mixed = pl.pallas_call(
        functools.partial(attend_kernel, vid),
        out_shape=jax.ShapeDtypeStruct((sources, rows + LSE_ROWS, HEAD), jnp.bfloat16),
        in_specs=[smem, vmem],
        out_specs=vmem,
        scratch_shapes=[
            VMEM((sources * rows, 2 * HEAD), jnp.bfloat16),
            VMEM((sources * rows, HEAD), jnp.bfloat16),
            VMEM((sources * rows, HEAD), jnp.bfloat16),
        ],
        compiler_params=pltpu.CompilerParams(vmem_limit_bytes=40 << 20),
        name="attend",
    )(text_lengths, moved)
    back = lax.all_to_all(mixed, "seq", 0, 0, tiled=True)
    attn_video, attn_text, lse_video, lse_text, proj_video = pl.pallas_call(
        functools.partial(project_kernel, functools.partial(place, w_out.shape[0])),
        out_shape=(
            jax.ShapeDtypeStruct((vid, feats), jnp.bfloat16),
            jax.ShapeDtypeStruct((txt, feats), jnp.bfloat16),
            jax.ShapeDtypeStruct((HEADS, 1, vid), jnp.float32),
            jax.ShapeDtypeStruct((txt, HEADS), jnp.float32),
            jax.ShapeDtypeStruct((vid, feats), jnp.bfloat16),
        ),
        in_specs=[vmem, vmem, smem, *[anywhere] * len(pieces)],
        out_specs=(vmem,) * 5,
        scratch_shapes=[VMEM((feats, feats), jnp.bfloat16), pltpu.SemaphoreType.DMA],
        compiler_params=pltpu.CompilerParams(vmem_limit_bytes=32 << 20),
        name="project",
    )(back, gate, spot, *pieces)
    return (
        attn_video[None],
        attn_text[None],
        lse_video.transpose(1, 0, 2),
        lse_text.T[None],
        proj_video[None],
    )


def solution(mesh):
    devices = mesh.devices.reshape(mesh.shape["seq"], *FSDP)
    mesh = Mesh(devices, ("seq", *FSDP_AXES))
    placed = (
        P(FSDP_AXES, "seq", None),
        P(FSDP_AXES, "seq", None, None),
        P(FSDP_AXES, "seq", None),
        P(FSDP_AXES, "seq", None, None),
        P(FSDP_AXES),
        P(FSDP_AXES, None),
        P(FSDP_AXES, None),
    )
    return jax.shard_map(
        functools.partial(shards, mesh.shape["seq"]),
        mesh=mesh,
        in_specs=placed,
        out_specs=(
            P(FSDP_AXES, "seq", None),
            P(FSDP_AXES, "seq", None),
            P(FSDP_AXES, None, "seq"),
            P(FSDP_AXES, None, "seq"),
            P(FSDP_AXES, "seq", None),
        ),
        check_vma=False,
    )
```

```python
import functools
import math

import jax
import jax.numpy as jnp
from jax import lax
from jax.experimental import pallas as pl
from jax.experimental.pallas import tpu as pltpu
from jax.sharding import Mesh
from jax.sharding import PartitionSpec as P

HEADS = 12
HEAD = 128
SLOPE = math.log2(math.e) / math.sqrt(HEAD)
LN2 = math.log(2.0)
LSE_ROWS = 16
SIZES = {"y": 8, "zl": 2, "zh": 4, "x": 4, "core": 2}
SEQ = ("y", "zl")
FSDP = ("zh", "x", "core")
GROUP = 4
VMEM = pltpu.VMEM


def pack_kernel(
    length_ref, base_ref, qv_hbm, kvv_hbm, qt_hbm, kvt_hbm, out_ref,
    qv_ref, kvv_ref, qt_ref, kvt_ref, split_ref, sems,
):
    vid = qv_ref.shape[0]
    txt = qt_ref.shape[0]
    pairs = ((kvv_hbm, kvv_ref), (kvt_hbm, kvt_ref), (qv_hbm, qv_ref), (qt_hbm, qt_ref))
    copies = [pltpu.make_async_copy(a, b, sems.at[i]) for i, (a, b) in enumerate(pairs)]
    for copy in copies:
        copy.start()
    for h in range(HEADS, out_ref.shape[0]):
        out_ref[h] = jnp.zeros(out_ref.shape[1:], jnp.bfloat16)
    copies[0].wait()
    copies[1].wait()
    slot = base_ref[0] + lax.broadcasted_iota(jnp.int32, (txt, HEAD), 0)
    valid = slot < length_ref[0]
    for h in range(HEADS):
        cols = pl.ds(h * HEAD, HEAD)
        video = kvv_ref[:, :, cols].astype(jnp.float32).reshape(2 * vid, HEAD)
        text = kvt_ref[:, :, cols].astype(jnp.float32).reshape(2 * txt, HEAD)
        split_ref[h, : 2 * vid] = video
        split_ref[h, 2 * vid :] = text
        keys = split_ref[h, pl.ds(0, vid, stride=2), :]
        text_keys = split_ref[h, pl.ds(2 * vid, txt, stride=2), :]
        text_values = split_ref[h, pl.ds(2 * vid + 1, txt, stride=2), :]
        out_ref[h, 1, :vid] = keys.astype(jnp.bfloat16)
        out_ref[h, 1, vid:] = jnp.where(valid, text_keys, keys[:1]).astype(jnp.bfloat16)
        out_ref[h, 2, :vid] = split_ref[h, pl.ds(1, vid, stride=2), :].astype(jnp.bfloat16)
        out_ref[h, 2, vid:] = jnp.where(valid, text_values, 0.0).astype(jnp.bfloat16)
    copies[2].wait()
    copies[3].wait()
    for h in range(HEADS):
        cols = pl.ds(h * HEAD, HEAD)
        out_ref[h, 0, :vid] = qv_ref[:, cols]
        out_ref[h, 0, vid:] = qt_ref[:, cols]


def attend_kernel(vid, length_ref, x_ref, out_ref, vals_ref, keys_ref, queries_ref):
    sources, _, rows, _ = x_ref.shape
    txt = rows - vid
    row = lax.broadcasted_iota(jnp.int32, (rows, HEAD), 0)
    for s in range(sources):
        valid = (row < vid) | (row - vid + s * txt < length_ref[0])
        here = pl.ds(s * rows, rows)
        queries_ref[here, :] = x_ref[s, 0]
        keys_ref[here, :] = x_ref[s, 1]
        vals_ref[here, :HEAD] = x_ref[s, 2]
        vals_ref[here, HEAD:] = jnp.where(valid, 1.0, 0.0).astype(jnp.bfloat16)

    def score(block):
        return lax.dot_general(
            queries_ref[pl.ds(block * GROUP * rows, GROUP * rows), :],
            keys_ref[...],
            (((1,), (1,)), ((), ())),
            preferred_element_type=jnp.float32,
        )

    blocks = sources // GROUP
    following = score(0)
    for block in range(blocks):
        scores = following
        if block + 1 < blocks:
            following = score(block + 1)
        best = jnp.max(scores, axis=1, keepdims=True) * SLOPE
        weights = jnp.exp2(scores * SLOPE - best).astype(jnp.bfloat16)
        both = jnp.dot(weights, vals_ref[...], preferred_element_type=jnp.float32)
        total = both[:, HEAD:]
        mixed = (both[:, :HEAD] / total).astype(jnp.bfloat16)
        wide = (best + jnp.log2(total)) * LN2
        for g in range(GROUP):
            s = block * GROUP + g
            out_ref[s, :rows] = mixed[g * rows : (g + 1) * rows]
            lse = wide[g * rows : (g + 1) * rows].T[:LSE_ROWS]
            high = lse.astype(jnp.bfloat16).astype(jnp.float32)
            mid = (lse - high).astype(jnp.bfloat16).astype(jnp.float32)
            which = lax.broadcasted_iota(jnp.int32, lse.shape, 0)
            parts = jnp.where(which == 0, high, jnp.where(which == 1, mid, lse - high - mid))
            out_ref[s, rows:] = parts.astype(jnp.bfloat16)


def project_kernel(
    x_ref, w_ref, more_ref, gate_ref, av_ref, at_ref, lv_ref, lt_ref, pv_ref
):
    vid = av_ref.shape[0]
    rows = vid + at_ref.shape[0]
    lses = []
    for h in range(HEADS):
        cols = pl.ds(h * HEAD, HEAD)
        av_ref[:, cols] = x_ref[h, :vid]
        at_ref[:, cols] = x_ref[h, vid:rows]
        parts = x_ref[h, rows:].astype(jnp.float32)
        lse = parts[0:1] + parts[1:2] + parts[2:3]
        lv_ref[h] = lse[:, :vid]
        lses.append(lse)
    lses += [lses[0]] * (HEAD - HEADS)
    lt_ref[...] = jnp.concatenate(lses, axis=0).T[vid:, :HEADS]
    split = w_ref.shape[1]
    for part, here in ((w_ref, pl.ds(0, split)), (more_ref, pl.ds(split, more_ref.shape[1]))):
        out = jnp.dot(av_ref[...], part[...], preferred_element_type=jnp.float32)
        pv_ref[:, here] = (out * gate_ref[:, here]).astype(jnp.bfloat16)


def order_kernel(count, spot_ref, *refs):
    *pieces, w_ref, more_ref = refs
    split = w_ref.shape[1]
    zl, zh, x, core = spot_ref[0], spot_ref[1], spot_ref[2], spot_ref[3]
    nz, nx = SIZES["zh"], SIZES["x"]
    near = 2 * zl - 1 + nz
    of_z = (zh, zh + near, zh + nz - near, zh + nz // 2)
    of_x = (x, x + nx - 1, x + 1, x + nx // 2)
    for i, piece in enumerate(pieces):
        which = i % len(of_x)
        for j in range(len(of_z)):
            row = (of_z[j] + nz) % nz * nx + (of_x[which]) % nx
            row = (row * SIZES["core"] + (core ^ (i // len(of_x)))) * count
            target = pl.ds(pl.multiple_of(row, 16), count)
            w_ref[target, :] = piece[pl.ds(j * count, count), :split]
            more_ref[target, :] = piece[pl.ds(j * count, count), split:]


def gathered(w_out):
    nz, nx = SIZES["zh"], SIZES["x"]
    between = []
    for zh in range(nz):
        here, there = nz + zh, (zh + 1) % nz
        between += [(here, there), (there, here)]
    first = lax.ppermute(w_out, ("zl", "zh"), between)
    second = lax.ppermute(first, "zl", [(0, 1), (1, 0)])
    third = lax.ppermute(second, ("zl", "zh"), between)
    column = jnp.concatenate([w_out, first, second, third], axis=0)
    up = [(i, (i + 1) % nx) for i in range(nx)]
    down = [(i, (i - 1) % nx) for i in range(nx)]
    left = lax.ppermute(column, "x", up)
    right = lax.ppermute(column, "x", down)
    half = column.shape[0] // 2
    far = [lax.ppermute(left[:half], "x", up), lax.ppermute(right[half:], "x", down)]
    mine = [column, left, right, jnp.concatenate(far, axis=0)]
    return mine + [lax.ppermute(part, "core", [(0, 1), (1, 0)]) for part in mine]


def shards(sources, q_video, kv_video, q_text, kv_text, text_lengths, gate, w_out):
    vid, feats = q_video.shape[1:]
    txt = q_text.shape[1]
    rows = vid + txt
    base = (lax.axis_index(SEQ) * txt).astype(jnp.int32).reshape(1)
    pieces = gathered(w_out)
    spot = jnp.stack([lax.axis_index(axis) for axis in ("zl", "zh", "x", "core")])
    smem = pl.BlockSpec(memory_space=pltpu.SMEM)
    vmem = pl.BlockSpec(memory_space=VMEM)
    anywhere = pl.BlockSpec(memory_space=pl.ANY)
    packed = pl.pallas_call(
        pack_kernel,
        out_shape=jax.ShapeDtypeStruct((sources, 3, rows, HEAD), jnp.bfloat16),
        in_specs=[smem, smem, anywhere, anywhere, anywhere, anywhere],
        out_specs=vmem,
        scratch_shapes=[
            VMEM((vid, feats), jnp.bfloat16),
            VMEM((vid, 2, feats), jnp.bfloat16),
            VMEM((txt, feats), jnp.bfloat16),
            VMEM((txt, 2, feats), jnp.bfloat16),
            VMEM((HEADS, 2 * rows, HEAD), jnp.float32),
            pltpu.SemaphoreType.DMA((4,)),
        ],
        compiler_params=pltpu.CompilerParams(vmem_limit_bytes=60 << 20),
        name="pack",
    )(
        text_lengths,
        base,
        q_video[0],
        kv_video[0],
        q_text[0],
        kv_text[0],
    )
    moved = lax.all_to_all(packed, SEQ, 0, 0, tiled=True)
    mixed = pl.pallas_call(
        functools.partial(attend_kernel, vid),
        out_shape=jax.ShapeDtypeStruct((sources, rows + LSE_ROWS, HEAD), jnp.bfloat16),
        in_specs=[smem, vmem],
        out_specs=vmem,
        scratch_shapes=[
            VMEM((sources * rows, 2 * HEAD), jnp.bfloat16),
            VMEM((sources * rows, HEAD), jnp.bfloat16),
            VMEM((sources * rows, HEAD), jnp.bfloat16),
        ],
        compiler_params=pltpu.CompilerParams(vmem_limit_bytes=40 << 20),
        name="attend",
    )(text_lengths, moved)
    back = lax.all_to_all(mixed, SEQ, 0, 0, tiled=True)
    halves = pl.pallas_call(
        functools.partial(order_kernel, w_out.shape[0]),
        out_shape=(jax.ShapeDtypeStruct((feats, feats // 2), jnp.bfloat16),) * 2,
        in_specs=[smem, *[vmem] * len(pieces)],
        out_specs=(vmem,) * 2,
        compiler_params=pltpu.CompilerParams(vmem_limit_bytes=32 << 20),
        name="order",
    )(spot.astype(jnp.int32), *pieces)
    attn_video, attn_text, lse_video, lse_text, proj_video = pl.pallas_call(
        project_kernel,
        out_shape=(
            jax.ShapeDtypeStruct((vid, feats), jnp.bfloat16),
            jax.ShapeDtypeStruct((txt, feats), jnp.bfloat16),
            jax.ShapeDtypeStruct((HEADS, 1, vid), jnp.float32),
            jax.ShapeDtypeStruct((txt, HEADS), jnp.float32),
            jax.ShapeDtypeStruct((vid, feats), jnp.bfloat16),
        ),
        in_specs=[vmem] * 4,
        out_specs=(vmem,) * 5,
        compiler_params=pltpu.CompilerParams(vmem_limit_bytes=32 << 20),
        name="project",
    )(back, *halves, gate)
    return (
        attn_video[None],
        attn_text[None],
        lse_video.transpose(1, 0, 2),
        lse_text.T[None],
        proj_video[None],
    )


def solution(mesh):
    sources = mesh.shape["seq"]
    mesh = Mesh(mesh.devices.reshape(tuple(SIZES.values())), tuple(SIZES))
    placed = (
        P(FSDP, SEQ, None),
        P(FSDP, SEQ, None, None),
        P(FSDP, SEQ, None),
        P(FSDP, SEQ, None, None),
        P(FSDP),
        P(FSDP, None),
        P(FSDP, None),
    )
    return jax.shard_map(
        functools.partial(shards, sources),
        mesh=mesh,
        in_specs=placed,
        out_specs=(
            P(FSDP, SEQ, None),
            P(FSDP, SEQ, None),
            P(FSDP, None, SEQ),
            P(FSDP, None, SEQ),
            P(FSDP, SEQ, None),
        ),
        check_vma=False,
    )
```

```python
import functools
import math

import jax
import jax.numpy as jnp
from jax import lax
from jax.experimental import pallas as pl
from jax.experimental.pallas import tpu as pltpu
from jax.sharding import Mesh
from jax.sharding import PartitionSpec as P

HEADS = 12
HEAD = 128
SLOPE = math.log2(math.e) / math.sqrt(HEAD)
LN2 = math.log(2.0)
LSE_ROWS = 16
SIZES = {"y": 8, "zl": 2, "zh": 4, "x": 4, "core": 2}
SEQ = ("y", "zl")
FSDP = ("zh", "x", "core")
GROUP = 4
VMEM = pltpu.VMEM


def pack_kernel(
    length_ref, base_ref, qv_hbm, kvv_hbm, qt_hbm, kvt_hbm, out_ref,
    qv_ref, kvv_ref, qt_ref, kvt_ref, split_ref, sems,
):
    vid = qv_ref.shape[0]
    txt = qt_ref.shape[0]
    pairs = ((kvv_hbm, kvv_ref), (kvt_hbm, kvt_ref), (qv_hbm, qv_ref), (qt_hbm, qt_ref))
    copies = [pltpu.make_async_copy(a, b, sems.at[i]) for i, (a, b) in enumerate(pairs)]
    for copy in copies:
        copy.start()
    for h in range(HEADS, out_ref.shape[0]):
        out_ref[h] = jnp.zeros(out_ref.shape[1:], jnp.bfloat16)
    copies[0].wait()
    copies[1].wait()
    slot = base_ref[0] + lax.broadcasted_iota(jnp.int32, (txt, HEAD), 0)
    valid = slot < length_ref[0]
    for h in range(HEADS):
        cols = pl.ds(h * HEAD, HEAD)
        video = kvv_ref[:, :, cols].astype(jnp.float32).reshape(2 * vid, HEAD)
        text = kvt_ref[:, :, cols].astype(jnp.float32).reshape(2 * txt, HEAD)
        split_ref[h, : 2 * vid] = video
        split_ref[h, 2 * vid :] = text
        keys = split_ref[h, pl.ds(0, vid, stride=2), :]
        text_keys = split_ref[h, pl.ds(2 * vid, txt, stride=2), :]
        text_values = split_ref[h, pl.ds(2 * vid + 1, txt, stride=2), :]
        out_ref[h, 1, :vid] = keys.astype(jnp.bfloat16)
        out_ref[h, 1, vid:] = jnp.where(valid, text_keys, keys[:1]).astype(jnp.bfloat16)
        out_ref[h, 2, :vid] = split_ref[h, pl.ds(1, vid, stride=2), :].astype(jnp.bfloat16)
        out_ref[h, 2, vid:] = jnp.where(valid, text_values, 0.0).astype(jnp.bfloat16)
    copies[2].wait()
    copies[3].wait()
    for h in range(HEADS):
        cols = pl.ds(h * HEAD, HEAD)
        out_ref[h, 0, :vid] = qv_ref[:, cols]
        out_ref[h, 0, vid:] = qt_ref[:, cols]


def attend_kernel(vid, length_ref, x_ref, out_ref, vals_ref, keys_ref, queries_ref):
    sources, _, rows, _ = x_ref.shape
    txt = rows - vid
    row = lax.broadcasted_iota(jnp.int32, (rows, HEAD), 0)
    for s in range(sources):
        valid = (row < vid) | (row - vid + s * txt < length_ref[0])
        here = pl.ds(s * rows, rows)
        queries_ref[here, :] = x_ref[s, 0]
        keys_ref[here, :] = x_ref[s, 1]
        vals_ref[here, :HEAD] = x_ref[s, 2]
        vals_ref[here, HEAD:] = jnp.where(valid, 1.0, 0.0).astype(jnp.bfloat16)

    def score(block):
        return lax.dot_general(
            queries_ref[pl.ds(block * GROUP * rows, GROUP * rows), :],
            keys_ref[...],
            (((1,), (1,)), ((), ())),
            preferred_element_type=jnp.float32,
        )

    blocks = sources // GROUP
    following = score(0)
    for block in range(blocks):
        scores = following
        if block + 1 < blocks:
            following = score(block + 1)
        best = jnp.max(scores, axis=1, keepdims=True) * SLOPE
        weights = jnp.exp2(scores * SLOPE - best).astype(jnp.bfloat16)
        both = jnp.dot(weights, vals_ref[...], preferred_element_type=jnp.float32)
        total = both[:, HEAD:]
        mixed = (both[:, :HEAD] / total).astype(jnp.bfloat16)
        wide = (best + jnp.log2(total)) * LN2
        for g in range(GROUP):
            s = block * GROUP + g
            out_ref[s, :rows] = mixed[g * rows : (g + 1) * rows]
            lse = wide[g * rows : (g + 1) * rows].T[:LSE_ROWS]
            high = lse.astype(jnp.bfloat16).astype(jnp.float32)
            mid = (lse - high).astype(jnp.bfloat16).astype(jnp.float32)
            which = lax.broadcasted_iota(jnp.int32, lse.shape, 0)
            parts = jnp.where(which == 0, high, jnp.where(which == 1, mid, lse - high - mid))
            out_ref[s, rows:] = parts.astype(jnp.bfloat16)


def project_kernel(
    spot_ref, x_ref, w_ref, other_ref, gate_ref, av_ref, at_ref, lv_ref, lt_ref, pv_ref
):
    vid = av_ref.shape[0]
    rows = vid + at_ref.shape[0]
    lses = []
    for h in range(HEADS):
        cols = pl.ds(h * HEAD, HEAD)
        av_ref[:, cols] = x_ref[h, :vid]
        at_ref[:, cols] = x_ref[h, vid:rows]
        parts = x_ref[h, rows:].astype(jnp.float32)
        lse = parts[0:1] + parts[1:2] + parts[2:3]
        lv_ref[h] = lse[:, :vid]
        lses.append(lse)
    lses += [lses[0]] * (HEAD - HEADS)
    lt_ref[...] = jnp.concatenate(lses, axis=0).T[vid:, :HEADS]
    blocks = SIZES["zh"] * SIZES["x"]
    mixed = av_ref[...].astype(jnp.float32)
    width = mixed.shape[1] // (blocks * SIZES["core"])
    even, odd = [
        jnp.concatenate(
            [mixed[:, (2 * i + c) * width : (2 * i + c + 1) * width] for i in range(blocks)], axis=1
        )
        for c in range(SIZES["core"])
    ]
    first = spot_ref[0] == 0
    mine = jnp.where(first, even, odd).astype(jnp.bfloat16)
    others = jnp.where(first, odd, even).astype(jnp.bfloat16)
    out = jnp.dot(mine, w_ref[...], preferred_element_type=jnp.float32)
    out += jnp.dot(others, other_ref[...], preferred_element_type=jnp.float32)
    pv_ref[...] = (out * gate_ref[...]).astype(jnp.bfloat16)


def shards(sources, q_video, kv_video, q_text, kv_text, text_lengths, gate, w_out):
    vid, feats = q_video.shape[1:]
    txt = q_text.shape[1]
    rows = vid + txt
    base = (lax.axis_index(SEQ) * txt).astype(jnp.int32).reshape(1)
    core = lax.axis_index("core")
    mine = lax.all_gather(w_out, ("zh", "x"), axis=0, tiled=True)
    smem = pl.BlockSpec(memory_space=pltpu.SMEM)
    vmem = pl.BlockSpec(memory_space=VMEM)
    anywhere = pl.BlockSpec(memory_space=pl.ANY)
    packed = pl.pallas_call(
        pack_kernel,
        out_shape=jax.ShapeDtypeStruct((sources, 3, rows, HEAD), jnp.bfloat16),
        in_specs=[smem, smem, anywhere, anywhere, anywhere, anywhere],
        out_specs=vmem,
        scratch_shapes=[
            VMEM((vid, feats), jnp.bfloat16),
            VMEM((vid, 2, feats), jnp.bfloat16),
            VMEM((txt, feats), jnp.bfloat16),
            VMEM((txt, 2, feats), jnp.bfloat16),
            VMEM((HEADS, 2 * rows, HEAD), jnp.float32),
            pltpu.SemaphoreType.DMA((4,)),
        ],
        compiler_params=pltpu.CompilerParams(vmem_limit_bytes=60 << 20),
        name="pack",
    )(
        text_lengths,
        base,
        q_video[0],
        kv_video[0],
        q_text[0],
        kv_text[0],
    )
    moved = lax.all_to_all(packed, SEQ, 0, 0, tiled=True)
    mixed = pl.pallas_call(
        functools.partial(attend_kernel, vid),
        out_shape=jax.ShapeDtypeStruct((sources, rows + LSE_ROWS, HEAD), jnp.bfloat16),
        in_specs=[smem, vmem],
        out_specs=vmem,
        scratch_shapes=[
            VMEM((sources * rows, 2 * HEAD), jnp.bfloat16),
            VMEM((sources * rows, HEAD), jnp.bfloat16),
            VMEM((sources * rows, HEAD), jnp.bfloat16),
        ],
        compiler_params=pltpu.CompilerParams(vmem_limit_bytes=40 << 20),
        name="attend",
    )(text_lengths, moved)
    after = lax.optimization_barrier((mine, mixed))[0]
    others = lax.ppermute(after, "core", [(0, 1), (1, 0)])
    back = lax.all_to_all(mixed, SEQ, 0, 0, tiled=True)
    attn_video, attn_text, lse_video, lse_text, proj_video = pl.pallas_call(
        project_kernel,
        out_shape=(
            jax.ShapeDtypeStruct((vid, feats), jnp.bfloat16),
            jax.ShapeDtypeStruct((txt, feats), jnp.bfloat16),
            jax.ShapeDtypeStruct((HEADS, 1, vid), jnp.float32),
            jax.ShapeDtypeStruct((txt, HEADS), jnp.float32),
            jax.ShapeDtypeStruct((vid, feats), jnp.bfloat16),
        ),
        in_specs=[smem, *[vmem] * 4],
        out_specs=(vmem,) * 5,
        compiler_params=pltpu.CompilerParams(vmem_limit_bytes=32 << 20),
        name="project",
    )(core.astype(jnp.int32).reshape(1), back, mine, others, gate)
    return (
        attn_video[None],
        attn_text[None],
        lse_video.transpose(1, 0, 2),
        lse_text.T[None],
        proj_video[None],
    )


def solution(mesh):
    sources = mesh.shape["seq"]
    mesh = Mesh(mesh.devices.reshape(tuple(SIZES.values())), tuple(SIZES))
    placed = (
        P(FSDP, SEQ, None),
        P(FSDP, SEQ, None, None),
        P(FSDP, SEQ, None),
        P(FSDP, SEQ, None, None),
        P(FSDP),
        P(FSDP, None),
        P(FSDP, None),
    )
    return jax.shard_map(
        functools.partial(shards, sources),
        mesh=mesh,
        in_specs=placed,
        out_specs=(
            P(FSDP, SEQ, None),
            P(FSDP, SEQ, None),
            P(FSDP, None, SEQ),
            P(FSDP, None, SEQ),
            P(FSDP, SEQ, None),
        ),
        check_vma=False,
    )
```

```python
import functools
import math

import jax
import jax.numpy as jnp
from jax import lax
from jax.experimental import pallas as pl
from jax.experimental.pallas import tpu as pltpu
from jax.sharding import Mesh
from jax.sharding import PartitionSpec as P

HEADS = 12
HEAD = 128
SLOPE = math.log2(math.e) / math.sqrt(HEAD)
LN2 = math.log(2.0)
LSE_ROWS = 16
SIZES = {"y": 8, "zl": 2, "zh": 4, "x": 4, "core": 2}
SEQ = ("y", "zl")
FSDP = ("zh", "x", "core")
GROUP = 4
VMEM = pltpu.VMEM


def pack_kernel(
    length_ref, base_ref, qv_hbm, kvv_hbm, qt_hbm, kvt_hbm, out_ref,
    qv_ref, kvv_ref, qt_ref, kvt_ref, split_ref, sems,
):
    vid = qv_ref.shape[0]
    txt = qt_ref.shape[0]
    pairs = ((kvv_hbm, kvv_ref), (kvt_hbm, kvt_ref), (qv_hbm, qv_ref), (qt_hbm, qt_ref))
    copies = [pltpu.make_async_copy(a, b, sems.at[i]) for i, (a, b) in enumerate(pairs)]
    for copy in copies:
        copy.start()
    for h in range(HEADS, out_ref.shape[0]):
        out_ref[h] = jnp.zeros(out_ref.shape[1:], jnp.bfloat16)
    copies[0].wait()
    copies[1].wait()
    slot = base_ref[0] + lax.broadcasted_iota(jnp.int32, (txt, HEAD), 0)
    valid = slot < length_ref[0]
    for h in range(HEADS):
        cols = pl.ds(h * HEAD, HEAD)
        video = kvv_ref[:, :, cols].astype(jnp.float32).reshape(2 * vid, HEAD)
        text = kvt_ref[:, :, cols].astype(jnp.float32).reshape(2 * txt, HEAD)
        split_ref[h, : 2 * vid] = video
        split_ref[h, 2 * vid :] = text
        keys = split_ref[h, pl.ds(0, vid, stride=2), :]
        text_keys = split_ref[h, pl.ds(2 * vid, txt, stride=2), :]
        text_values = split_ref[h, pl.ds(2 * vid + 1, txt, stride=2), :]
        out_ref[h, 1, :vid] = keys.astype(jnp.bfloat16)
        out_ref[h, 1, vid:] = jnp.where(valid, text_keys, keys[:1]).astype(jnp.bfloat16)
        out_ref[h, 2, :vid] = split_ref[h, pl.ds(1, vid, stride=2), :].astype(jnp.bfloat16)
        out_ref[h, 2, vid:] = jnp.where(valid, text_values, 0.0).astype(jnp.bfloat16)
    copies[2].wait()
    copies[3].wait()
    for h in range(HEADS):
        cols = pl.ds(h * HEAD, HEAD)
        out_ref[h, 0, :vid] = qv_ref[:, cols]
        out_ref[h, 0, vid:] = qt_ref[:, cols]


def attend_kernel(vid, length_ref, x_ref, out_ref, vals_ref, keys_ref, queries_ref):
    sources, _, rows, _ = x_ref.shape
    txt = rows - vid
    row = lax.broadcasted_iota(jnp.int32, (rows, HEAD), 0)
    for s in range(sources):
        valid = (row < vid) | (row - vid + s * txt < length_ref[0])
        here = pl.ds(s * rows, rows)
        queries_ref[here, :] = x_ref[s, 0]
        keys_ref[here, :] = x_ref[s, 1]
        vals_ref[here, :HEAD] = x_ref[s, 2]
        vals_ref[here, HEAD:] = jnp.where(valid, 1.0, 0.0).astype(jnp.bfloat16)

    def score(block):
        return lax.dot_general(
            queries_ref[pl.ds(block * GROUP * rows, GROUP * rows), :],
            keys_ref[...],
            (((1,), (1,)), ((), ())),
            preferred_element_type=jnp.float32,
        )

    blocks = sources // GROUP
    following = score(0)
    for block in range(blocks):
        scores = following
        if block + 1 < blocks:
            following = score(block + 1)
        best = jnp.max(scores, axis=1, keepdims=True) * SLOPE
        weights = jnp.exp2(scores * SLOPE - best).astype(jnp.bfloat16)
        both = jnp.dot(weights, vals_ref[...], preferred_element_type=jnp.float32)
        total = both[:, HEAD:]
        mixed = (both[:, :HEAD] / total).astype(jnp.bfloat16)
        wide = (best + jnp.log2(total)) * LN2
        for g in range(GROUP):
            s = block * GROUP + g
            out_ref[s, :rows] = mixed[g * rows : (g + 1) * rows]
            lse = wide[g * rows : (g + 1) * rows].T[:LSE_ROWS]
            high = lse.astype(jnp.bfloat16).astype(jnp.float32)
            mid = (lse - high).astype(jnp.bfloat16).astype(jnp.float32)
            which = lax.broadcasted_iota(jnp.int32, lse.shape, 0)
            parts = jnp.where(which == 0, high, jnp.where(which == 1, mid, lse - high - mid))
            out_ref[s, rows:] = parts.astype(jnp.bfloat16)


def project_kernel(
    spot_ref, x_ref, w_ref, gate_ref, av_ref, at_ref, lv_ref, lt_ref, half_ref, mixed_ref
):
    vid = av_ref.shape[0]
    rows = vid + at_ref.shape[0]
    lses = []
    for h in range(HEADS):
        cols = pl.ds(h * HEAD, HEAD)
        av_ref[:, cols] = x_ref[h, :vid]
        at_ref[:, cols] = x_ref[h, vid:rows]
        parts = x_ref[h, rows:].astype(jnp.float32)
        lse = parts[0:1] + parts[1:2] + parts[2:3]
        lv_ref[h] = lse[:, :vid]
        lses.append(lse)
    lses += [lses[0]] * (HEAD - HEADS)
    lt_ref[...] = jnp.concatenate(lses, axis=0).T[vid:, :HEADS]
    nz, nx = SIZES["zh"], SIZES["x"]
    mixed = av_ref[...].astype(jnp.float32)
    width = mixed.shape[1] // (nz * nx)
    mixed = jnp.concatenate(
        [mixed[:, (z * nx + x) * width :][:, :width] for x in range(nx) for z in range(nz)], axis=1
    ).astype(jnp.bfloat16)
    mixed_ref[...] = mixed
    half = w_ref.shape[1]
    here = pl.ds(pl.multiple_of(spot_ref[0] * half, half), half)
    out = jnp.dot(mixed, w_ref[...], preferred_element_type=jnp.float32)
    half_ref[...] = (out * gate_ref[:, here]).astype(jnp.bfloat16)


def finish_kernel(spot_ref, mixed_ref, w_ref, gate_ref, half_ref, pv_ref):
    half = w_ref.shape[1]
    near = pl.ds(pl.multiple_of(spot_ref[0] * half, half), half)
    here = pl.ds(pl.multiple_of((1 - spot_ref[0]) * half, half), half)
    pv_ref[:, near] = half_ref[...]
    out = jnp.dot(mixed_ref[...], w_ref[...], preferred_element_type=jnp.float32)
    pv_ref[:, here] = (out * gate_ref[:, here]).astype(jnp.bfloat16)


def shards(sources, q_video, kv_video, q_text, kv_text, text_lengths, gate, w_out):
    vid, feats = q_video.shape[1:]
    txt = q_text.shape[1]
    rows = vid + txt
    base = (lax.axis_index(SEQ) * txt).astype(jnp.int32).reshape(1)
    core = lax.axis_index("core")
    spot = core.astype(jnp.int32).reshape(1)
    along_z = lax.all_gather(w_out, ("zh", "core"), axis=0, tiled=True)
    smem = pl.BlockSpec(memory_space=pltpu.SMEM)
    vmem = pl.BlockSpec(memory_space=VMEM)
    anywhere = pl.BlockSpec(memory_space=pl.ANY)
    packed = pl.pallas_call(
        pack_kernel,
        out_shape=jax.ShapeDtypeStruct((sources, 3, rows, HEAD), jnp.bfloat16),
        in_specs=[smem, smem, anywhere, anywhere, anywhere, anywhere],
        out_specs=vmem,
        scratch_shapes=[
            VMEM((vid, feats), jnp.bfloat16),
            VMEM((vid, 2, feats), jnp.bfloat16),
            VMEM((txt, feats), jnp.bfloat16),
            VMEM((txt, 2, feats), jnp.bfloat16),
            VMEM((HEADS, 2 * rows, HEAD), jnp.float32),
            pltpu.SemaphoreType.DMA((4,)),
        ],
        compiler_params=pltpu.CompilerParams(vmem_limit_bytes=60 << 20),
        name="pack",
    )(
        text_lengths,
        base,
        q_video[0],
        kv_video[0],
        q_text[0],
        kv_text[0],
    )
    moved = lax.all_to_all(packed, SEQ, 0, 0, tiled=True)
    half = feats // SIZES["core"]
    along_z = lax.optimization_barrier((along_z, moved))[0]
    mine = lax.dynamic_slice_in_dim(along_z, core * half, half, axis=1)
    mine = lax.all_gather(mine, "x", axis=0, tiled=True)
    mixed = pl.pallas_call(
        functools.partial(attend_kernel, vid),
        out_shape=jax.ShapeDtypeStruct((sources, rows + LSE_ROWS, HEAD), jnp.bfloat16),
        in_specs=[smem, vmem],
        out_specs=vmem,
        scratch_shapes=[
            VMEM((sources * rows, 2 * HEAD), jnp.bfloat16),
            VMEM((sources * rows, HEAD), jnp.bfloat16),
            VMEM((sources * rows, HEAD), jnp.bfloat16),
        ],
        compiler_params=pltpu.CompilerParams(vmem_limit_bytes=40 << 20),
        name="attend",
    )(text_lengths, moved)
    back = lax.all_to_all(mixed, SEQ, 0, 0, tiled=True)
    mine, back = lax.optimization_barrier((mine, back))
    others = lax.ppermute(mine, "core", [(0, 1), (1, 0)])
    attn_video, attn_text, lse_video, lse_text, part, ordered = pl.pallas_call(
        project_kernel,
        out_shape=(
            jax.ShapeDtypeStruct((vid, feats), jnp.bfloat16),
            jax.ShapeDtypeStruct((txt, feats), jnp.bfloat16),
            jax.ShapeDtypeStruct((HEADS, 1, vid), jnp.float32),
            jax.ShapeDtypeStruct((txt, HEADS), jnp.float32),
            jax.ShapeDtypeStruct((vid, half), jnp.bfloat16),
            jax.ShapeDtypeStruct((vid, feats), jnp.bfloat16),
        ),
        in_specs=[smem, *[vmem] * 3],
        out_specs=(vmem,) * 6,
        compiler_params=pltpu.CompilerParams(vmem_limit_bytes=32 << 20),
        name="project",
    )(spot, back, mine, gate)
    proj_video = pl.pallas_call(
        finish_kernel,
        out_shape=jax.ShapeDtypeStruct((vid, feats), jnp.bfloat16),
        in_specs=[smem, *[vmem] * 4],
        out_specs=vmem,
        compiler_params=pltpu.CompilerParams(vmem_limit_bytes=32 << 20),
        name="finish",
    )(spot, ordered, others, gate, part)
    return (
        attn_video[None],
        attn_text[None],
        lse_video.transpose(1, 0, 2),
        lse_text.T[None],
        proj_video[None],
    )


def solution(mesh):
    sources = mesh.shape["seq"]
    mesh = Mesh(mesh.devices.reshape(tuple(SIZES.values())), tuple(SIZES))
    placed = (
        P(FSDP, SEQ, None),
        P(FSDP, SEQ, None, None),
        P(FSDP, SEQ, None),
        P(FSDP, SEQ, None, None),
        P(FSDP),
        P(FSDP, None),
        P(FSDP, None),
    )
    return jax.shard_map(
        functools.partial(shards, sources),
        mesh=mesh,
        in_specs=placed,
        out_specs=(
            P(FSDP, SEQ, None),
            P(FSDP, SEQ, None),
            P(FSDP, None, SEQ),
            P(FSDP, None, SEQ),
            P(FSDP, SEQ, None),
        ),
        check_vma=False,
    )
```

```python
import functools
import math

import jax
import jax.numpy as jnp
from jax import lax
from jax.experimental import pallas as pl
from jax.experimental.pallas import tpu as pltpu
from jax.sharding import Mesh
from jax.sharding import PartitionSpec as P

HEADS = 12
HEAD = 128
SLOPE = math.log2(math.e) / math.sqrt(HEAD)
LN2 = math.log(2.0)
LSE_ROWS = 16
SIZES = {"y": 8, "zl": 2, "zh": 4, "x": 4, "core": 2}
SEQ = ("y", "zl")
FSDP = ("zh", "x", "core")
GROUP = 4
VMEM = pltpu.VMEM


def pack_kernel(
    length_ref, base_ref, qv_hbm, kvv_hbm, qt_hbm, kvt_hbm, out_ref,
    qv_ref, kvv_ref, qt_ref, kvt_ref, split_ref, sems,
):
    vid = qv_ref.shape[0]
    txt = qt_ref.shape[0]
    pairs = ((kvv_hbm, kvv_ref), (kvt_hbm, kvt_ref), (qv_hbm, qv_ref), (qt_hbm, qt_ref))
    copies = [pltpu.make_async_copy(a, b, sems.at[i]) for i, (a, b) in enumerate(pairs)]
    for copy in copies:
        copy.start()
    for h in range(HEADS, out_ref.shape[0]):
        out_ref[h] = jnp.zeros(out_ref.shape[1:], jnp.bfloat16)
    copies[0].wait()
    copies[1].wait()
    slot = base_ref[0] + lax.broadcasted_iota(jnp.int32, (txt, HEAD), 0)
    valid = slot < length_ref[0]
    for h in range(HEADS):
        cols = pl.ds(h * HEAD, HEAD)
        video = kvv_ref[:, :, cols].astype(jnp.float32).reshape(2 * vid, HEAD)
        text = kvt_ref[:, :, cols].astype(jnp.float32).reshape(2 * txt, HEAD)
        split_ref[h, : 2 * vid] = video
        split_ref[h, 2 * vid :] = text
        keys = split_ref[h, pl.ds(0, vid, stride=2), :]
        text_keys = split_ref[h, pl.ds(2 * vid, txt, stride=2), :]
        text_values = split_ref[h, pl.ds(2 * vid + 1, txt, stride=2), :]
        out_ref[h, 1, :vid] = keys.astype(jnp.bfloat16)
        out_ref[h, 1, vid:] = jnp.where(valid, text_keys, keys[:1]).astype(jnp.bfloat16)
        out_ref[h, 2, :vid] = split_ref[h, pl.ds(1, vid, stride=2), :].astype(jnp.bfloat16)
        out_ref[h, 2, vid:] = jnp.where(valid, text_values, 0.0).astype(jnp.bfloat16)
    copies[2].wait()
    copies[3].wait()
    for h in range(HEADS):
        cols = pl.ds(h * HEAD, HEAD)
        out_ref[h, 0, :vid] = qv_ref[:, cols]
        out_ref[h, 0, vid:] = qt_ref[:, cols]


def attend_kernel(vid, length_ref, x_ref, out_ref, vals_ref, keys_ref, queries_ref):
    sources, _, rows, _ = x_ref.shape
    txt = rows - vid
    row = lax.broadcasted_iota(jnp.int32, (rows, HEAD), 0)
    for s in range(sources):
        valid = (row < vid) | (row - vid + s * txt < length_ref[0])
        here = pl.ds(s * rows, rows)
        queries_ref[here, :] = x_ref[s, 0]
        keys_ref[here, :] = x_ref[s, 1]
        vals_ref[here, :HEAD] = x_ref[s, 2]
        vals_ref[here, HEAD:] = jnp.where(valid, 1.0, 0.0).astype(jnp.bfloat16)

    def score(block):
        return lax.dot_general(
            queries_ref[pl.ds(block * GROUP * rows, GROUP * rows), :],
            keys_ref[...],
            (((1,), (1,)), ((), ())),
            preferred_element_type=jnp.float32,
        )

    blocks = sources // GROUP
    following = score(0)
    for block in range(blocks):
        scores = following
        if block + 1 < blocks:
            following = score(block + 1)
        best = jnp.max(scores, axis=1, keepdims=True) * SLOPE
        weights = jnp.exp2(scores * SLOPE - best).astype(jnp.bfloat16)
        both = jnp.dot(weights, vals_ref[...], preferred_element_type=jnp.float32)
        total = both[:, HEAD:]
        mixed = (both[:, :HEAD] / total).astype(jnp.bfloat16)
        wide = (best + jnp.log2(total)) * LN2
        for g in range(GROUP):
            s = block * GROUP + g
            out_ref[s, :rows] = mixed[g * rows : (g + 1) * rows]
            lse = wide[g * rows : (g + 1) * rows].T[:LSE_ROWS]
            high = lse.astype(jnp.bfloat16).astype(jnp.float32)
            mid = (lse - high).astype(jnp.bfloat16).astype(jnp.float32)
            which = lax.broadcasted_iota(jnp.int32, lse.shape, 0)
            parts = jnp.where(which == 0, high, jnp.where(which == 1, mid, lse - high - mid))
            out_ref[s, rows:] = parts.astype(jnp.bfloat16)


def project_kernel(
    x_ref, w_ref, more_ref, gate_ref, av_ref, at_ref, lv_ref, lt_ref, pv_ref
):
    vid = av_ref.shape[0]
    rows = vid + at_ref.shape[0]
    lses = []
    for h in range(HEADS):
        cols = pl.ds(h * HEAD, HEAD)
        av_ref[:, cols] = x_ref[h, :vid]
        at_ref[:, cols] = x_ref[h, vid:rows]
        parts = x_ref[h, rows:].astype(jnp.float32)
        lse = parts[0:1] + parts[1:2] + parts[2:3]
        lv_ref[h] = lse[:, :vid]
        lses.append(lse)
    lses += [lses[0]] * (HEAD - HEADS)
    lt_ref[...] = jnp.concatenate(lses, axis=0).T[vid:, :HEADS]
    split = w_ref.shape[1]
    for part, here in ((w_ref, pl.ds(0, split)), (more_ref, pl.ds(split, more_ref.shape[1]))):
        out = jnp.dot(av_ref[...], part[...], preferred_element_type=jnp.float32)
        pv_ref[:, here] = (out * gate_ref[:, here]).astype(jnp.bfloat16)


def order_kernel(count, spot_ref, *refs):
    *pieces, w_ref, more_ref = refs
    split = w_ref.shape[1]
    zl, zh, x, core = spot_ref[0], spot_ref[1], spot_ref[2], spot_ref[3]
    nz, nx = SIZES["zh"], SIZES["x"]
    near = 2 * zl - 1 + nz
    of_z = (zh, zh + near, zh + nz - near, zh + nz // 2)
    of_x = (x, x + nx - 1, x + 1, x + nx // 2)
    for i, piece in enumerate(pieces):
        which = i % len(of_x)
        for j in range(len(of_z)):
            row = (of_z[j] + nz) % nz * nx + (of_x[which]) % nx
            row = (row * SIZES["core"] + (core ^ (i // len(of_x)))) * count
            target = pl.ds(pl.multiple_of(row, 16), count)
            w_ref[target, :] = piece[pl.ds(j * count, count), :split]
            more_ref[target, :] = piece[pl.ds(j * count, count), split:]


def across(block):
    nz = SIZES["zh"]
    between = []
    for zh in range(nz):
        here, there = nz + zh, (zh + 1) % nz
        between += [(here, there), (there, here)]
    return lax.ppermute(block, ("zl", "zh"), between)


def gathered(w_out, first, second):
    nx = SIZES["x"]
    column = jnp.concatenate([w_out, first, second, across(second)], axis=0)
    up = [(i, (i + 1) % nx) for i in range(nx)]
    down = [(i, (i - 1) % nx) for i in range(nx)]
    left = lax.ppermute(column, "x", up)
    right = lax.ppermute(column, "x", down)
    half = column.shape[0] // 2
    far = [lax.ppermute(left[:half], "x", up), lax.ppermute(right[half:], "x", down)]
    mine = [column, left, right, jnp.concatenate(far, axis=0)]
    return mine + [lax.ppermute(part, "core", [(0, 1), (1, 0)]) for part in mine]


def shards(sources, q_video, kv_video, q_text, kv_text, text_lengths, gate, w_out):
    vid, feats = q_video.shape[1:]
    txt = q_text.shape[1]
    rows = vid + txt
    base = (lax.axis_index(SEQ) * txt).astype(jnp.int32).reshape(1)
    first = across(w_out)
    second = lax.ppermute(first, "zl", [(0, 1), (1, 0)])
    pieces = gathered(w_out, first, second)
    spot = jnp.stack([lax.axis_index(axis) for axis in ("zl", "zh", "x", "core")])
    smem = pl.BlockSpec(memory_space=pltpu.SMEM)
    vmem = pl.BlockSpec(memory_space=VMEM)
    anywhere = pl.BlockSpec(memory_space=pl.ANY)
    packed = pl.pallas_call(
        pack_kernel,
        out_shape=jax.ShapeDtypeStruct((sources, 3, rows, HEAD), jnp.bfloat16),
        in_specs=[smem, smem, anywhere, anywhere, anywhere, anywhere],
        out_specs=vmem,
        scratch_shapes=[
            VMEM((vid, feats), jnp.bfloat16),
            VMEM((vid, 2, feats), jnp.bfloat16),
            VMEM((txt, feats), jnp.bfloat16),
            VMEM((txt, 2, feats), jnp.bfloat16),
            VMEM((HEADS, 2 * rows, HEAD), jnp.float32),
            pltpu.SemaphoreType.DMA((4,)),
        ],
        compiler_params=pltpu.CompilerParams(vmem_limit_bytes=60 << 20),
        name="pack",
    )(
        text_lengths,
        base,
        q_video[0],
        kv_video[0],
        q_text[0],
        kv_text[0],
    )
    packed = lax.optimization_barrier((packed, second))[0]
    moved = lax.all_to_all(packed, SEQ, 0, 0, tiled=True)
    mixed = pl.pallas_call(
        functools.partial(attend_kernel, vid),
        out_shape=jax.ShapeDtypeStruct((sources, rows + LSE_ROWS, HEAD), jnp.bfloat16),
        in_specs=[smem, vmem],
        out_specs=vmem,
        scratch_shapes=[
            VMEM((sources * rows, 2 * HEAD), jnp.bfloat16),
            VMEM((sources * rows, HEAD), jnp.bfloat16),
            VMEM((sources * rows, HEAD), jnp.bfloat16),
        ],
        compiler_params=pltpu.CompilerParams(vmem_limit_bytes=40 << 20),
        name="attend",
    )(text_lengths, moved)
    back = lax.all_to_all(mixed, SEQ, 0, 0, tiled=True)
    halves = pl.pallas_call(
        functools.partial(order_kernel, w_out.shape[0]),
        out_shape=(jax.ShapeDtypeStruct((feats, feats // 2), jnp.bfloat16),) * 2,
        in_specs=[smem, *[vmem] * len(pieces)],
        out_specs=(vmem,) * 2,
        compiler_params=pltpu.CompilerParams(vmem_limit_bytes=32 << 20),
        name="order",
    )(spot.astype(jnp.int32), *pieces)
    attn_video, attn_text, lse_video, lse_text, proj_video = pl.pallas_call(
        project_kernel,
        out_shape=(
            jax.ShapeDtypeStruct((vid, feats), jnp.bfloat16),
            jax.ShapeDtypeStruct((txt, feats), jnp.bfloat16),
            jax.ShapeDtypeStruct((HEADS, 1, vid), jnp.float32),
            jax.ShapeDtypeStruct((txt, HEADS), jnp.float32),
            jax.ShapeDtypeStruct((vid, feats), jnp.bfloat16),
        ),
        in_specs=[vmem] * 4,
        out_specs=(vmem,) * 5,
        compiler_params=pltpu.CompilerParams(vmem_limit_bytes=32 << 20),
        name="project",
    )(back, *halves, gate)
    return (
        attn_video[None],
        attn_text[None],
        lse_video.transpose(1, 0, 2),
        lse_text.T[None],
        proj_video[None],
    )


def solution(mesh):
    sources = mesh.shape["seq"]
    mesh = Mesh(mesh.devices.reshape(tuple(SIZES.values())), tuple(SIZES))
    placed = (
        P(FSDP, SEQ, None),
        P(FSDP, SEQ, None, None),
        P(FSDP, SEQ, None),
        P(FSDP, SEQ, None, None),
        P(FSDP),
        P(FSDP, None),
        P(FSDP, None),
    )
    return jax.shard_map(
        functools.partial(shards, sources),
        mesh=mesh,
        in_specs=placed,
        out_specs=(
            P(FSDP, SEQ, None),
            P(FSDP, SEQ, None),
            P(FSDP, None, SEQ),
            P(FSDP, None, SEQ),
            P(FSDP, SEQ, None),
        ),
        check_vma=False,
    )
```

```python
import functools
import math

import jax
import jax.numpy as jnp
from jax import lax
from jax.experimental import pallas as pl
from jax.experimental.pallas import tpu as pltpu
from jax.sharding import Mesh
from jax.sharding import PartitionSpec as P

HEADS = 12
HEAD = 128
SLOPE = math.log2(math.e) / math.sqrt(HEAD)
LN2 = math.log(2.0)
LSE_ROWS = 16
SIZES = {"y": 8, "zl": 2, "zh": 4, "x": 4, "core": 2}
SEQ = ("y", "zl")
FSDP = ("zh", "x", "core")
GROUP = 4
VMEM = pltpu.VMEM


def pack_kernel(
    length_ref, base_ref, qv_hbm, kvv_hbm, qt_hbm, kvt_hbm, out_ref,
    qv_ref, kvv_ref, qt_ref, kvt_ref, split_ref, sems,
):
    vid = qv_ref.shape[0]
    txt = qt_ref.shape[0]
    pairs = ((kvv_hbm, kvv_ref), (kvt_hbm, kvt_ref), (qv_hbm, qv_ref), (qt_hbm, qt_ref))
    copies = [pltpu.make_async_copy(a, b, sems.at[i]) for i, (a, b) in enumerate(pairs)]
    for copy in copies:
        copy.start()
    for h in range(HEADS, out_ref.shape[0]):
        out_ref[h] = jnp.zeros(out_ref.shape[1:], jnp.bfloat16)
    copies[0].wait()
    copies[1].wait()
    slot = base_ref[0] + lax.broadcasted_iota(jnp.int32, (txt, HEAD), 0)
    valid = slot < length_ref[0]
    for h in range(HEADS):
        cols = pl.ds(h * HEAD, HEAD)
        video = kvv_ref[:, :, cols].astype(jnp.float32).reshape(2 * vid, HEAD)
        text = kvt_ref[:, :, cols].astype(jnp.float32).reshape(2 * txt, HEAD)
        split_ref[h, : 2 * vid] = video
        split_ref[h, 2 * vid :] = text
        keys = split_ref[h, pl.ds(0, vid, stride=2), :]
        text_keys = split_ref[h, pl.ds(2 * vid, txt, stride=2), :]
        text_values = split_ref[h, pl.ds(2 * vid + 1, txt, stride=2), :]
        out_ref[h, 1, :vid] = keys.astype(jnp.bfloat16)
        out_ref[h, 1, vid:] = jnp.where(valid, text_keys, keys[:1]).astype(jnp.bfloat16)
        out_ref[h, 2, :vid] = split_ref[h, pl.ds(1, vid, stride=2), :].astype(jnp.bfloat16)
        out_ref[h, 2, vid:] = jnp.where(valid, text_values, 0.0).astype(jnp.bfloat16)
    copies[2].wait()
    copies[3].wait()
    for h in range(HEADS):
        cols = pl.ds(h * HEAD, HEAD)
        out_ref[h, 0, :vid] = qv_ref[:, cols]
        out_ref[h, 0, vid:] = qt_ref[:, cols]


def attend_kernel(vid, length_ref, x_ref, out_ref, vals_ref, keys_ref, queries_ref):
    sources, _, rows, _ = x_ref.shape
    txt = rows - vid
    row = lax.broadcasted_iota(jnp.int32, (rows, HEAD), 0)
    for s in range(sources):
        valid = (row < vid) | (row - vid + s * txt < length_ref[0])
        here = pl.ds(s * rows, rows)
        queries_ref[here, :] = x_ref[s, 0]
        keys_ref[here, :] = x_ref[s, 1]
        vals_ref[here, :HEAD] = x_ref[s, 2]
        vals_ref[here, HEAD:] = jnp.where(valid, 1.0, 0.0).astype(jnp.bfloat16)

    def score(block):
        return lax.dot_general(
            queries_ref[pl.ds(block * GROUP * rows, GROUP * rows), :],
            keys_ref[...],
            (((1,), (1,)), ((), ())),
            preferred_element_type=jnp.float32,
        )

    blocks = sources // GROUP
    following = score(0)
    for block in range(blocks):
        scores = following
        if block + 1 < blocks:
            following = score(block + 1)
        best = jnp.max(scores, axis=1, keepdims=True) * SLOPE
        weights = jnp.exp2(scores * SLOPE - best).astype(jnp.bfloat16)
        both = jnp.dot(weights, vals_ref[...], preferred_element_type=jnp.float32)
        total = both[:, HEAD:]
        mixed = (both[:, :HEAD] / total).astype(jnp.bfloat16)
        wide = (best + jnp.log2(total)) * LN2
        for g in range(GROUP):
            s = block * GROUP + g
            out_ref[s, :rows] = mixed[g * rows : (g + 1) * rows]
            lse = wide[g * rows : (g + 1) * rows].T[:LSE_ROWS]
            high = lse.astype(jnp.bfloat16).astype(jnp.float32)
            mid = (lse - high).astype(jnp.bfloat16).astype(jnp.float32)
            which = lax.broadcasted_iota(jnp.int32, lse.shape, 0)
            parts = jnp.where(which == 0, high, jnp.where(which == 1, mid, lse - high - mid))
            out_ref[s, rows:] = parts.astype(jnp.bfloat16)


def project_kernel(spot_ref, x_ref, gate_ref, *refs):
    pieces = refs[:8]
    av_ref, at_ref, lv_ref, lt_ref, pv_ref, turned_ref, mixed_ref = refs[8:]
    vid = av_ref.shape[0]
    rows = vid + at_ref.shape[0]
    lses = []
    for h in range(HEADS):
        cols = pl.ds(h * HEAD, HEAD)
        av_ref[:, cols] = x_ref[h, :vid]
        at_ref[:, cols] = x_ref[h, vid:rows]
        turned_ref[cols, :] = x_ref[h, :rows].astype(jnp.float32).T.astype(jnp.bfloat16)
        parts = x_ref[h, rows:].astype(jnp.float32)
        lse = parts[0:1] + parts[1:2] + parts[2:3]
        lv_ref[h] = lse[:, :vid]
        lses.append(lse)
    lses += [lses[0]] * (HEAD - HEADS)
    lt_ref[...] = jnp.concatenate(lses, axis=0).T[vid:, :HEADS]

    zl, zh, x, core = spot_ref[0], spot_ref[1], spot_ref[2], spot_ref[3]
    nz, nx = SIZES["zh"], SIZES["x"]
    near = 2 * zl - 1 + nz
    of_z = (zh, zh + near, zh + nz - near, zh + nz // 2)
    of_x = (x, x + nx - 1, x + 1, x + nx // 2)
    depth = pieces[0].shape[0]
    count = depth // nz
    for i in range(len(pieces)):
        for j in range(nz):
            row = (of_z[j] + nz) % nz * nx + of_x[i % nx] % nx
            row = (row * SIZES["core"] + (core ^ (i // nx))) * count
            source = pl.ds(pl.multiple_of(row, 16), count)
            mixed_ref[pl.ds(i * depth + j * count, count), :] = turned_ref[source, :]
    mixed = mixed_ref[...].astype(jnp.float32).T[:vid].astype(jnp.bfloat16)
    width = 512
    for first in range(0, pv_ref.shape[1], width):
        here = pl.ds(first, width)
        out = jnp.zeros((vid, width), jnp.float32)
        for i, piece in enumerate(pieces):
            out += jnp.dot(
                mixed[:, i * depth : (i + 1) * depth], piece[:, here], preferred_element_type=jnp.float32
            )
        pv_ref[:, here] = (out * gate_ref[:, here]).astype(jnp.bfloat16)


def across(block):
    nz = SIZES["zh"]
    between = []
    for zh in range(nz):
        here, there = nz + zh, (zh + 1) % nz
        between += [(here, there), (there, here)]
    return lax.ppermute(block, ("zl", "zh"), between)


def gathered(w_out, first, second):
    nx = SIZES["x"]
    column = jnp.concatenate([w_out, first, second, across(second)], axis=0)
    up = [(i, (i + 1) % nx) for i in range(nx)]
    down = [(i, (i - 1) % nx) for i in range(nx)]
    left = lax.ppermute(column, "x", up)
    right = lax.ppermute(column, "x", down)
    half = column.shape[0] // 2
    far = [lax.ppermute(left[:half], "x", up), lax.ppermute(right[half:], "x", down)]
    mine = [column, left, right, jnp.concatenate(far, axis=0)]
    return mine + [lax.ppermute(part, "core", [(0, 1), (1, 0)]) for part in mine]


def shards(sources, q_video, kv_video, q_text, kv_text, text_lengths, gate, w_out):
    vid, feats = q_video.shape[1:]
    txt = q_text.shape[1]
    rows = vid + txt
    base = (lax.axis_index(SEQ) * txt).astype(jnp.int32).reshape(1)
    first = across(w_out)
    second = lax.ppermute(first, "zl", [(0, 1), (1, 0)])
    pieces = gathered(w_out, first, second)
    spot = jnp.stack([lax.axis_index(axis) for axis in ("zl", "zh", "x", "core")])
    smem = pl.BlockSpec(memory_space=pltpu.SMEM)
    vmem = pl.BlockSpec(memory_space=VMEM)
    anywhere = pl.BlockSpec(memory_space=pl.ANY)
    packed = pl.pallas_call(
        pack_kernel,
        out_shape=jax.ShapeDtypeStruct((sources, 3, rows, HEAD), jnp.bfloat16),
        in_specs=[smem, smem, anywhere, anywhere, anywhere, anywhere],
        out_specs=vmem,
        scratch_shapes=[
            VMEM((vid, feats), jnp.bfloat16),
            VMEM((vid, 2, feats), jnp.bfloat16),
            VMEM((txt, feats), jnp.bfloat16),
            VMEM((txt, 2, feats), jnp.bfloat16),
            VMEM((HEADS, 2 * rows, HEAD), jnp.float32),
            pltpu.SemaphoreType.DMA((4,)),
        ],
        compiler_params=pltpu.CompilerParams(vmem_limit_bytes=60 << 20),
        name="pack",
    )(
        text_lengths,
        base,
        q_video[0],
        kv_video[0],
        q_text[0],
        kv_text[0],
    )
    packed = lax.optimization_barrier((packed, second))[0]
    moved = lax.all_to_all(packed, SEQ, 0, 0, tiled=True)
    mixed = pl.pallas_call(
        functools.partial(attend_kernel, vid),
        out_shape=jax.ShapeDtypeStruct((sources, rows + LSE_ROWS, HEAD), jnp.bfloat16),
        in_specs=[smem, vmem],
        out_specs=vmem,
        scratch_shapes=[
            VMEM((sources * rows, 2 * HEAD), jnp.bfloat16),
            VMEM((sources * rows, HEAD), jnp.bfloat16),
            VMEM((sources * rows, HEAD), jnp.bfloat16),
        ],
        compiler_params=pltpu.CompilerParams(vmem_limit_bytes=40 << 20),
        name="attend",
    )(text_lengths, moved)
    back = lax.all_to_all(mixed, SEQ, 0, 0, tiled=True)
    attn_video, attn_text, lse_video, lse_text, proj_video = pl.pallas_call(
        project_kernel,
        out_shape=(
            jax.ShapeDtypeStruct((vid, feats), jnp.bfloat16),
            jax.ShapeDtypeStruct((txt, feats), jnp.bfloat16),
            jax.ShapeDtypeStruct((HEADS, 1, vid), jnp.float32),
            jax.ShapeDtypeStruct((txt, HEADS), jnp.float32),
            jax.ShapeDtypeStruct((vid, feats), jnp.bfloat16),
        ),
        in_specs=[smem, *[vmem] * (2 + len(pieces))],
        out_specs=(vmem,) * 5,
        scratch_shapes=[VMEM((feats, rows), jnp.bfloat16)] * 2,
        compiler_params=pltpu.CompilerParams(vmem_limit_bytes=16 << 20),
        name="project",
    )(spot.astype(jnp.int32), back, gate, *pieces)
    return (
        attn_video[None],
        attn_text[None],
        lse_video.transpose(1, 0, 2),
        lse_text.T[None],
        proj_video[None],
    )


def solution(mesh):
    sources = mesh.shape["seq"]
    mesh = Mesh(mesh.devices.reshape(tuple(SIZES.values())), tuple(SIZES))
    placed = (
        P(FSDP, SEQ, None),
        P(FSDP, SEQ, None, None),
        P(FSDP, SEQ, None),
        P(FSDP, SEQ, None, None),
        P(FSDP),
        P(FSDP, None),
        P(FSDP, None),
    )
    return jax.shard_map(
        functools.partial(shards, sources),
        mesh=mesh,
        in_specs=placed,
        out_specs=(
            P(FSDP, SEQ, None),
            P(FSDP, SEQ, None),
            P(FSDP, None, SEQ),
            P(FSDP, None, SEQ),
            P(FSDP, SEQ, None),
        ),
        check_vma=False,
    )
```

```python
import functools
import math

import jax
import jax.numpy as jnp
from jax import lax
from jax.experimental import pallas as pl
from jax.experimental.pallas import tpu as pltpu
from jax.sharding import Mesh
from jax.sharding import PartitionSpec as P

HEADS = 12
HEAD = 128
SLOPE = math.log2(math.e) / math.sqrt(HEAD)
LN2 = math.log(2.0)
LSE_ROWS = 16
SIZES = {"y": 8, "zl": 2, "zh": 4, "x": 4, "core": 2}
SEQ = ("y", "zl")
FSDP = ("zh", "x", "core")
GROUP = 4
VMEM = pltpu.VMEM


def pack_kernel(
    length_ref, base_ref, qv_hbm, kvv_hbm, qt_hbm, kvt_hbm, out_ref,
    qv_ref, kvv_ref, qt_ref, kvt_ref, split_ref, sems,
):
    vid = qv_ref.shape[0]
    txt = qt_ref.shape[0]
    pairs = ((kvv_hbm, kvv_ref), (kvt_hbm, kvt_ref), (qv_hbm, qv_ref), (qt_hbm, qt_ref))
    copies = [pltpu.make_async_copy(a, b, sems.at[i]) for i, (a, b) in enumerate(pairs)]
    for copy in copies:
        copy.start()
    for h in range(HEADS, out_ref.shape[0]):
        out_ref[h] = jnp.zeros(out_ref.shape[1:], jnp.bfloat16)
    copies[0].wait()
    copies[1].wait()
    slot = base_ref[0] + lax.broadcasted_iota(jnp.int32, (txt, HEAD), 0)
    valid = slot < length_ref[0]
    for h in range(HEADS):
        cols = pl.ds(h * HEAD, HEAD)
        video = kvv_ref[:, :, cols].astype(jnp.float32).reshape(2 * vid, HEAD)
        text = kvt_ref[:, :, cols].astype(jnp.float32).reshape(2 * txt, HEAD)
        split_ref[h, : 2 * vid] = video
        split_ref[h, 2 * vid :] = text
        keys = split_ref[h, pl.ds(0, vid, stride=2), :]
        text_keys = split_ref[h, pl.ds(2 * vid, txt, stride=2), :]
        text_values = split_ref[h, pl.ds(2 * vid + 1, txt, stride=2), :]
        out_ref[h, 1, :vid] = keys.astype(jnp.bfloat16)
        out_ref[h, 1, vid:] = jnp.where(valid, text_keys, keys[:1]).astype(jnp.bfloat16)
        out_ref[h, 2, :vid] = split_ref[h, pl.ds(1, vid, stride=2), :].astype(jnp.bfloat16)
        out_ref[h, 2, vid:] = jnp.where(valid, text_values, 0.0).astype(jnp.bfloat16)
    copies[2].wait()
    copies[3].wait()
    for h in range(HEADS):
        cols = pl.ds(h * HEAD, HEAD)
        out_ref[h, 0, :vid] = qv_ref[:, cols]
        out_ref[h, 0, vid:] = qt_ref[:, cols]


def attend_kernel(vid, length_ref, x_ref, out_ref, vals_ref, keys_ref, queries_ref):
    sources, _, rows, _ = x_ref.shape
    txt = rows - vid
    row = lax.broadcasted_iota(jnp.int32, (rows, HEAD), 0)
    for s in range(sources):
        valid = (row < vid) | (row - vid + s * txt < length_ref[0])
        here = pl.ds(s * rows, rows)
        queries_ref[here, :] = x_ref[s, 0]
        keys_ref[here, :] = x_ref[s, 1]
        vals_ref[here, :HEAD] = x_ref[s, 2]
        vals_ref[here, HEAD:] = jnp.where(valid, 1.0, 0.0).astype(jnp.bfloat16)

    def score(block):
        return lax.dot_general(
            queries_ref[pl.ds(block * GROUP * rows, GROUP * rows), :],
            keys_ref[...],
            (((1,), (1,)), ((), ())),
            preferred_element_type=jnp.float32,
        )

    blocks = sources // GROUP
    following = score(0)
    for block in range(blocks):
        scores = following
        if block + 1 < blocks:
            following = score(block + 1)
        best = jnp.max(scores, axis=1, keepdims=True) * SLOPE
        weights = jnp.exp2(scores * SLOPE - best).astype(jnp.bfloat16)
        both = jnp.dot(weights, vals_ref[...], preferred_element_type=jnp.float32)
        total = both[:, HEAD:]
        mixed = (both[:, :HEAD] / total).astype(jnp.bfloat16)
        wide = (best + jnp.log2(total)) * LN2
        for g in range(GROUP):
            s = block * GROUP + g
            out_ref[s, :rows] = mixed[g * rows : (g + 1) * rows]
            lse = wide[g * rows : (g + 1) * rows].T[:LSE_ROWS]
            high = lse.astype(jnp.bfloat16).astype(jnp.float32)
            mid = (lse - high).astype(jnp.bfloat16).astype(jnp.float32)
            which = lax.broadcasted_iota(jnp.int32, lse.shape, 0)
            parts = jnp.where(which == 0, high, jnp.where(which == 1, mid, lse - high - mid))
            out_ref[s, rows:] = parts.astype(jnp.bfloat16)


def project_kernel(spot_ref, x_ref, gate_ref, *refs):
    pieces = refs[:8]
    av_ref, at_ref, lv_ref, lt_ref, pv_ref, turned_ref, mixed_ref = refs[8:]
    vid = av_ref.shape[0]
    rows = vid + at_ref.shape[0]
    lses = []
    for h in range(HEADS):
        cols = pl.ds(h * HEAD, HEAD)
        av_ref[:, cols] = x_ref[h, :vid]
        at_ref[:, cols] = x_ref[h, vid:rows]
        turned_ref[cols, :] = x_ref[h, :rows].astype(jnp.float32).T.astype(jnp.bfloat16)
        parts = x_ref[h, rows:].astype(jnp.float32)
        lse = parts[0:1] + parts[1:2] + parts[2:3]
        lv_ref[h] = lse[:, :vid]
        lses.append(lse)
    lses += [lses[0]] * (HEAD - HEADS)
    lt_ref[...] = jnp.concatenate(lses, axis=0).T[vid:, :HEADS]

    zl, zh, x, core = spot_ref[0], spot_ref[1], spot_ref[2], spot_ref[3]
    nz, nx = SIZES["zh"], SIZES["x"]
    near = 2 * zl - 1 + nz
    of_z = (zh, zh + near, zh + nz - near, zh + nz // 2)
    of_x = (x, x + nx - 1, x + 1, x + nx // 2)
    depth = pieces[0].shape[0]
    count = depth // nz
    for i in range(len(pieces)):
        for j in range(nz):
            row = (of_z[j] + nz) % nz * nx + of_x[i % nx] % nx
            row = (row * SIZES["core"] + (core ^ (i // nx))) * count
            source = pl.ds(pl.multiple_of(row, 16), count)
            mixed_ref[pl.ds(i * depth + j * count, count), :] = turned_ref[source, :]
    mixed = mixed_ref[...].astype(jnp.float32).T[:vid].astype(jnp.bfloat16)
    width = 512
    for first in range(0, pv_ref.shape[1], width):
        here = pl.ds(first, width)
        out = jnp.zeros((vid, width), jnp.float32)
        for i, piece in enumerate(pieces):
            out += jnp.dot(
                mixed[:, i * depth : (i + 1) * depth], piece[:, here], preferred_element_type=jnp.float32
            )
        pv_ref[:, here] = (out * gate_ref[:, here]).astype(jnp.bfloat16)


def across(block):
    nz = SIZES["zh"]
    between = []
    for zh in range(nz):
        here, there = nz + zh, (zh + 1) % nz
        between += [(here, there), (there, here)]
    return lax.ppermute(block, ("zl", "zh"), between)


def gathered(w_out, first, second):
    nx = SIZES["x"]
    column = jnp.concatenate([w_out, first, second, across(second)], axis=0)
    up = [(i, (i + 1) % nx) for i in range(nx)]
    down = [(i, (i - 1) % nx) for i in range(nx)]
    left = lax.ppermute(column, "x", up)
    right = lax.ppermute(column, "x", down)
    half = column.shape[0] // 2
    far = [lax.ppermute(left[:half], "x", up), lax.ppermute(right[half:], "x", down)]
    mine = [column, left, right, jnp.concatenate(far, axis=0)]
    return mine + [lax.ppermute(part, "core", [(0, 1), (1, 0)]) for part in mine]


def shards(sources, q_video, kv_video, q_text, kv_text, text_lengths, gate, w_out):
    vid, feats = q_video.shape[1:]
    txt = q_text.shape[1]
    rows = vid + txt
    base = (lax.axis_index(SEQ) * txt).astype(jnp.int32).reshape(1)
    first = across(w_out)
    second = lax.ppermute(first, "zl", [(0, 1), (1, 0)])
    pieces = gathered(w_out, first, second)
    spot = jnp.stack([lax.axis_index(axis) for axis in ("zl", "zh", "x", "core")])
    smem = pl.BlockSpec(memory_space=pltpu.SMEM)
    vmem = pl.BlockSpec(memory_space=VMEM)
    anywhere = pl.BlockSpec(memory_space=pl.ANY)
    packed = pl.pallas_call(
        pack_kernel,
        out_shape=jax.ShapeDtypeStruct((sources, 3, rows, HEAD), jnp.bfloat16),
        in_specs=[smem, smem, anywhere, anywhere, anywhere, anywhere],
        out_specs=vmem,
        scratch_shapes=[
            VMEM((vid, feats), jnp.bfloat16),
            VMEM((vid, 2, feats), jnp.bfloat16),
            VMEM((txt, feats), jnp.bfloat16),
            VMEM((txt, 2, feats), jnp.bfloat16),
            VMEM((HEADS, 2 * rows, HEAD), jnp.float32),
            pltpu.SemaphoreType.DMA((4,)),
        ],
        compiler_params=pltpu.CompilerParams(vmem_limit_bytes=60 << 20),
        name="pack",
    )(
        text_lengths,
        base,
        q_video[0],
        kv_video[0],
        q_text[0],
        kv_text[0],
    )
    packed = lax.optimization_barrier((packed, first))[0]
    moved = lax.all_to_all(packed, SEQ, 0, 0, tiled=True)
    mixed = pl.pallas_call(
        functools.partial(attend_kernel, vid),
        out_shape=jax.ShapeDtypeStruct((sources, rows + LSE_ROWS, HEAD), jnp.bfloat16),
        in_specs=[smem, vmem],
        out_specs=vmem,
        scratch_shapes=[
            VMEM((sources * rows, 2 * HEAD), jnp.bfloat16),
            VMEM((sources * rows, HEAD), jnp.bfloat16),
            VMEM((sources * rows, HEAD), jnp.bfloat16),
        ],
        compiler_params=pltpu.CompilerParams(vmem_limit_bytes=40 << 20),
        name="attend",
    )(text_lengths, moved)
    back = lax.all_to_all(mixed, SEQ, 0, 0, tiled=True)
    attn_video, attn_text, lse_video, lse_text, proj_video = pl.pallas_call(
        project_kernel,
        out_shape=(
            jax.ShapeDtypeStruct((vid, feats), jnp.bfloat16),
            jax.ShapeDtypeStruct((txt, feats), jnp.bfloat16),
            jax.ShapeDtypeStruct((HEADS, 1, vid), jnp.float32),
            jax.ShapeDtypeStruct((txt, HEADS), jnp.float32),
            jax.ShapeDtypeStruct((vid, feats), jnp.bfloat16),
        ),
        in_specs=[smem, *[vmem] * (2 + len(pieces))],
        out_specs=(vmem,) * 5,
        scratch_shapes=[VMEM((feats, rows), jnp.bfloat16)] * 2,
        compiler_params=pltpu.CompilerParams(vmem_limit_bytes=16 << 20),
        name="project",
    )(spot.astype(jnp.int32), back, gate, *pieces)
    return (
        attn_video[None],
        attn_text[None],
        lse_video.transpose(1, 0, 2),
        lse_text.T[None],
        proj_video[None],
    )


def solution(mesh):
    sources = mesh.shape["seq"]
    mesh = Mesh(mesh.devices.reshape(tuple(SIZES.values())), tuple(SIZES))
    placed = (
        P(FSDP, SEQ, None),
        P(FSDP, SEQ, None, None),
        P(FSDP, SEQ, None),
        P(FSDP, SEQ, None, None),
        P(FSDP),
        P(FSDP, None),
        P(FSDP, None),
    )
    return jax.shard_map(
        functools.partial(shards, sources),
        mesh=mesh,
        in_specs=placed,
        out_specs=(
            P(FSDP, SEQ, None),
            P(FSDP, SEQ, None),
            P(FSDP, None, SEQ),
            P(FSDP, None, SEQ),
            P(FSDP, SEQ, None),
        ),
        check_vma=False,
    )
```

```python
import functools
import math

import jax
import jax.numpy as jnp
from jax import lax
from jax.experimental import pallas as pl
from jax.experimental.pallas import tpu as pltpu
from jax.sharding import Mesh
from jax.sharding import PartitionSpec as P

HEADS = 12
HEAD = 128
SLOPE = math.log2(math.e) / math.sqrt(HEAD)
LN2 = math.log(2.0)
LSE_ROWS = 16
SIZES = {"y": 8, "zl": 2, "zh": 4, "x": 4, "core": 2}
SEQ = ("y", "zl")
FSDP = ("zh", "x", "core")
GROUP = 4
WIDTH = 512
VMEM = pltpu.VMEM


def pack_kernel(
    length_ref, base_ref, qv_hbm, kvv_hbm, qt_hbm, kvt_hbm, out_ref,
    qv_ref, kvv_ref, qt_ref, kvt_ref, split_ref, sems,
):
    vid = qv_ref.shape[0]
    txt = qt_ref.shape[0]
    pairs = ((kvv_hbm, kvv_ref), (kvt_hbm, kvt_ref), (qv_hbm, qv_ref), (qt_hbm, qt_ref))
    copies = [pltpu.make_async_copy(a, b, sems.at[i]) for i, (a, b) in enumerate(pairs)]
    for copy in copies:
        copy.start()
    for h in range(HEADS, out_ref.shape[0]):
        out_ref[h] = jnp.zeros(out_ref.shape[1:], jnp.bfloat16)
    copies[0].wait()
    copies[1].wait()
    slot = base_ref[0] + lax.broadcasted_iota(jnp.int32, (txt, HEAD), 0)
    valid = slot < length_ref[0]
    for h in range(HEADS):
        cols = pl.ds(h * HEAD, HEAD)
        video = kvv_ref[:, :, cols].astype(jnp.float32).reshape(2 * vid, HEAD)
        text = kvt_ref[:, :, cols].astype(jnp.float32).reshape(2 * txt, HEAD)
        split_ref[h, : 2 * vid] = video
        split_ref[h, 2 * vid :] = text
        keys = split_ref[h, pl.ds(0, vid, stride=2), :]
        text_keys = split_ref[h, pl.ds(2 * vid, txt, stride=2), :]
        text_values = split_ref[h, pl.ds(2 * vid + 1, txt, stride=2), :]
        out_ref[h, 1, :vid] = keys.astype(jnp.bfloat16)
        out_ref[h, 1, vid:] = jnp.where(valid, text_keys, keys[:1]).astype(jnp.bfloat16)
        out_ref[h, 2, :vid] = split_ref[h, pl.ds(1, vid, stride=2), :].astype(jnp.bfloat16)
        out_ref[h, 2, vid:] = jnp.where(valid, text_values, 0.0).astype(jnp.bfloat16)
    copies[2].wait()
    copies[3].wait()
    for h in range(HEADS):
        cols = pl.ds(h * HEAD, HEAD)
        out_ref[h, 0, :vid] = qv_ref[:, cols]
        out_ref[h, 0, vid:] = qt_ref[:, cols]


def attend_kernel(vid, length_ref, x_ref, out_ref, vals_ref, keys_ref, queries_ref):
    sources, _, rows, _ = x_ref.shape
    txt = rows - vid
    row = lax.broadcasted_iota(jnp.int32, (rows, HEAD), 0)
    for s in range(sources):
        valid = (row < vid) | (row - vid + s * txt < length_ref[0])
        here = pl.ds(s * rows, rows)
        queries_ref[here, :] = x_ref[s, 0]
        keys_ref[here, :] = x_ref[s, 1]
        vals_ref[here, :HEAD] = x_ref[s, 2]
        vals_ref[here, HEAD:] = jnp.where(valid, 1.0, 0.0).astype(jnp.bfloat16)

    def score(block):
        return lax.dot_general(
            queries_ref[pl.ds(block * GROUP * rows, GROUP * rows), :],
            keys_ref[...],
            (((1,), (1,)), ((), ())),
            preferred_element_type=jnp.float32,
        )

    blocks = sources // GROUP
    following = score(0)
    for block in range(blocks):
        scores = following
        if block + 1 < blocks:
            following = score(block + 1)
        best = jnp.max(scores, axis=1, keepdims=True) * SLOPE
        weights = jnp.exp2(scores * SLOPE - best).astype(jnp.bfloat16)
        both = jnp.dot(weights, vals_ref[...], preferred_element_type=jnp.float32)
        total = both[:, HEAD:]
        mixed = (both[:, :HEAD] / total).astype(jnp.bfloat16)
        wide = (best + jnp.log2(total)) * LN2
        for g in range(GROUP):
            s = block * GROUP + g
            out_ref[s, :rows] = mixed[g * rows : (g + 1) * rows]
            lse = wide[g * rows : (g + 1) * rows].T[:LSE_ROWS]
            high = lse.astype(jnp.bfloat16).astype(jnp.float32)
            mid = (lse - high).astype(jnp.bfloat16).astype(jnp.float32)
            which = lax.broadcasted_iota(jnp.int32, lse.shape, 0)
            parts = jnp.where(which == 0, high, jnp.where(which == 1, mid, lse - high - mid))
            out_ref[s, rows:] = parts.astype(jnp.bfloat16)


def project_kernel(spot_ref, x_ref, gate_ref, *refs):
    pieces, swapped = refs[:4], refs[4:8]
    av_ref, at_ref, lv_ref, lt_ref, pv_ref = refs[8:13]
    turned_ref, mixed_ref, held_ref, total_ref, sems = refs[13:]
    copies = [
        pltpu.make_async_copy(piece, held_ref.at[i], sems.at[i]) for i, piece in enumerate(swapped)
    ]
    for copy in copies:
        copy.start()
    vid = av_ref.shape[0]
    rows = vid + at_ref.shape[0]
    lses = []
    for h in range(HEADS):
        cols = pl.ds(h * HEAD, HEAD)
        av_ref[:, cols] = x_ref[h, :vid]
        at_ref[:, cols] = x_ref[h, vid:rows]
        turned_ref[cols, :] = x_ref[h, :rows].astype(jnp.float32).T.astype(jnp.bfloat16)
        parts = x_ref[h, rows:].astype(jnp.float32)
        lse = parts[0:1] + parts[1:2] + parts[2:3]
        lv_ref[h] = lse[:, :vid]
        lses.append(lse)
    lses += [lses[0]] * (HEAD - HEADS)
    lt_ref[...] = jnp.concatenate(lses, axis=0).T[vid:, :HEADS]

    zl, zh, x, core = spot_ref[0], spot_ref[1], spot_ref[2], spot_ref[3]
    nz, nx = SIZES["zh"], SIZES["x"]
    near = 2 * zl - 1 + nz
    of_z = (zh, zh + near, zh + nz - near, zh + nz // 2)
    of_x = (x, x + nx - 1, x + 1, x + nx // 2)
    depth = pieces[0].shape[0]
    count = depth // nz
    for i in range(len(pieces) + len(swapped)):
        for j in range(nz):
            row = (of_z[j] + nz) % nz * nx + of_x[i % nx] % nx
            row = (row * SIZES["core"] + (core ^ (i // nx))) * count
            source = pl.ds(pl.multiple_of(row, 16), count)
            mixed_ref[pl.ds(i * depth + j * count, count), :] = turned_ref[source, :]
    mixed = mixed_ref[...].astype(jnp.float32).T[:vid].astype(jnp.bfloat16)
    starts = range(0, pv_ref.shape[1], WIDTH)
    for first in starts:
        here = pl.ds(first, WIDTH)
        total_ref[:, here] = sum(
            jnp.dot(
                mixed[:, i * depth : (i + 1) * depth], piece[:, here], preferred_element_type=jnp.float32
            )
            for i, piece in enumerate(pieces)
        )
    for copy in copies:
        copy.wait()
    rest = mixed[:, len(pieces) * depth :]
    for first in starts:
        here = pl.ds(first, WIDTH)
        out = total_ref[:, here] + sum(
            jnp.dot(
                rest[:, i * depth : (i + 1) * depth],
                held_ref[i, :, here],
                preferred_element_type=jnp.float32,
            )
            for i in range(len(swapped))
        )
        pv_ref[:, here] = (out * gate_ref[:, here]).astype(jnp.bfloat16)


def across(block):
    nz = SIZES["zh"]
    between = []
    for zh in range(nz):
        here, there = nz + zh, (zh + 1) % nz
        between += [(here, there), (there, here)]
    return lax.ppermute(block, ("zl", "zh"), between)


def gathered(w_out, first, second):
    nx = SIZES["x"]
    column = jnp.concatenate([w_out, first, second, across(second)], axis=0)
    up = [(i, (i + 1) % nx) for i in range(nx)]
    down = [(i, (i - 1) % nx) for i in range(nx)]
    left = lax.ppermute(column, "x", up)
    right = lax.ppermute(column, "x", down)
    half = column.shape[0] // 2
    far = [lax.ppermute(left[:half], "x", up), lax.ppermute(right[half:], "x", down)]
    mine = [column, left, right, jnp.concatenate(far, axis=0)]
    return mine + [lax.ppermute(part, "core", [(0, 1), (1, 0)]) for part in mine]


def shards(sources, q_video, kv_video, q_text, kv_text, text_lengths, gate, w_out):
    vid, feats = q_video.shape[1:]
    txt = q_text.shape[1]
    rows = vid + txt
    base = (lax.axis_index(SEQ) * txt).astype(jnp.int32).reshape(1)
    first = across(w_out)
    second = lax.ppermute(first, "zl", [(0, 1), (1, 0)])
    pieces = gathered(w_out, first, second)
    spot = jnp.stack([lax.axis_index(axis) for axis in ("zl", "zh", "x", "core")])
    smem = pl.BlockSpec(memory_space=pltpu.SMEM)
    vmem = pl.BlockSpec(memory_space=VMEM)
    anywhere = pl.BlockSpec(memory_space=pl.ANY)
    packed = pl.pallas_call(
        pack_kernel,
        out_shape=jax.ShapeDtypeStruct((sources, 3, rows, HEAD), jnp.bfloat16),
        in_specs=[smem, smem, anywhere, anywhere, anywhere, anywhere],
        out_specs=vmem,
        scratch_shapes=[
            VMEM((vid, feats), jnp.bfloat16),
            VMEM((vid, 2, feats), jnp.bfloat16),
            VMEM((txt, feats), jnp.bfloat16),
            VMEM((txt, 2, feats), jnp.bfloat16),
            VMEM((HEADS, 2 * rows, HEAD), jnp.float32),
            pltpu.SemaphoreType.DMA((4,)),
        ],
        compiler_params=pltpu.CompilerParams(vmem_limit_bytes=60 << 20),
        name="pack",
    )(
        text_lengths,
        base,
        q_video[0],
        kv_video[0],
        q_text[0],
        kv_text[0],
    )
    packed = lax.optimization_barrier((packed, first))[0]
    moved = lax.all_to_all(packed, SEQ, 0, 0, tiled=True)
    mixed = pl.pallas_call(
        functools.partial(attend_kernel, vid),
        out_shape=jax.ShapeDtypeStruct((sources, rows + LSE_ROWS, HEAD), jnp.bfloat16),
        in_specs=[smem, vmem],
        out_specs=vmem,
        scratch_shapes=[
            VMEM((sources * rows, 2 * HEAD), jnp.bfloat16),
            VMEM((sources * rows, HEAD), jnp.bfloat16),
            VMEM((sources * rows, HEAD), jnp.bfloat16),
        ],
        compiler_params=pltpu.CompilerParams(vmem_limit_bytes=40 << 20),
        name="attend",
    )(text_lengths, moved)
    back = lax.all_to_all(mixed, SEQ, 0, 0, tiled=True)
    attn_video, attn_text, lse_video, lse_text, proj_video = pl.pallas_call(
        project_kernel,
        out_shape=(
            jax.ShapeDtypeStruct((vid, feats), jnp.bfloat16),
            jax.ShapeDtypeStruct((txt, feats), jnp.bfloat16),
            jax.ShapeDtypeStruct((HEADS, 1, vid), jnp.float32),
            jax.ShapeDtypeStruct((txt, HEADS), jnp.float32),
            jax.ShapeDtypeStruct((vid, feats), jnp.bfloat16),
        ),
        in_specs=[smem, *[vmem] * 6, *[anywhere] * 4],
        out_specs=(vmem,) * 5,
        scratch_shapes=[
            VMEM((feats, rows), jnp.bfloat16),
            VMEM((feats, rows), jnp.bfloat16),
            VMEM((4, *pieces[0].shape), jnp.bfloat16),
            VMEM((vid, feats), jnp.float32),
            pltpu.SemaphoreType.DMA((4,)),
        ],
        compiler_params=pltpu.CompilerParams(vmem_limit_bytes=16 << 20),
        name="project",
    )(spot.astype(jnp.int32), back, gate, *pieces)
    return (
        attn_video[None],
        attn_text[None],
        lse_video.transpose(1, 0, 2),
        lse_text.T[None],
        proj_video[None],
    )


def solution(mesh):
    sources = mesh.shape["seq"]
    mesh = Mesh(mesh.devices.reshape(tuple(SIZES.values())), tuple(SIZES))
    placed = (
        P(FSDP, SEQ, None),
        P(FSDP, SEQ, None, None),
        P(FSDP, SEQ, None),
        P(FSDP, SEQ, None, None),
        P(FSDP),
        P(FSDP, None),
        P(FSDP, None),
    )
    return jax.shard_map(
        functools.partial(shards, sources),
        mesh=mesh,
        in_specs=placed,
        out_specs=(
            P(FSDP, SEQ, None),
            P(FSDP, SEQ, None),
            P(FSDP, None, SEQ),
            P(FSDP, None, SEQ),
            P(FSDP, SEQ, None),
        ),
        check_vma=False,
    )
```

```python
import functools
import math

import jax
import jax.numpy as jnp
from jax import lax
from jax.experimental import pallas as pl
from jax.experimental.pallas import tpu as pltpu
from jax.sharding import Mesh
from jax.sharding import PartitionSpec as P

HEADS = 12
HEAD = 128
SLOPE = math.log2(math.e) / math.sqrt(HEAD)
LN2 = math.log(2.0)
LSE_ROWS = 16
SIZES = {"y": 8, "zl": 2, "zh": 4, "x": 4, "core": 2}
SEQ = ("y", "zl")
FSDP = ("zh", "x", "core")
GROUP = 4
VMEM = pltpu.VMEM


def pack_kernel(
    length_ref, base_ref, qv_hbm, kvv_hbm, qt_hbm, kvt_hbm, out_ref,
    qv_ref, kvv_ref, qt_ref, kvt_ref, split_ref, sems,
):
    vid = qv_ref.shape[0]
    txt = qt_ref.shape[0]
    pairs = ((kvv_hbm, kvv_ref), (kvt_hbm, kvt_ref), (qv_hbm, qv_ref), (qt_hbm, qt_ref))
    copies = [pltpu.make_async_copy(a, b, sems.at[i]) for i, (a, b) in enumerate(pairs)]
    for copy in copies:
        copy.start()
    for h in range(HEADS, out_ref.shape[0]):
        out_ref[h] = jnp.zeros(out_ref.shape[1:], jnp.bfloat16)
    copies[0].wait()
    copies[1].wait()
    slot = base_ref[0] + lax.broadcasted_iota(jnp.int32, (txt, HEAD), 0)
    valid = slot < length_ref[0]
    for h in range(HEADS):
        cols = pl.ds(h * HEAD, HEAD)
        video = kvv_ref[:, :, cols].astype(jnp.float32).reshape(2 * vid, HEAD)
        text = kvt_ref[:, :, cols].astype(jnp.float32).reshape(2 * txt, HEAD)
        split_ref[h, : 2 * vid] = video
        split_ref[h, 2 * vid :] = text
        keys = split_ref[h, pl.ds(0, vid, stride=2), :]
        text_keys = split_ref[h, pl.ds(2 * vid, txt, stride=2), :]
        text_values = split_ref[h, pl.ds(2 * vid + 1, txt, stride=2), :]
        out_ref[h, 1, :vid] = keys.astype(jnp.bfloat16)
        out_ref[h, 1, vid:] = jnp.where(valid, text_keys, keys[:1]).astype(jnp.bfloat16)
        out_ref[h, 2, :vid] = split_ref[h, pl.ds(1, vid, stride=2), :].astype(jnp.bfloat16)
        out_ref[h, 2, vid:] = jnp.where(valid, text_values, 0.0).astype(jnp.bfloat16)
    copies[2].wait()
    copies[3].wait()
    for h in range(HEADS):
        cols = pl.ds(h * HEAD, HEAD)
        out_ref[h, 0, :vid] = qv_ref[:, cols]
        out_ref[h, 0, vid:] = qt_ref[:, cols]


def attend_kernel(vid, length_ref, x_ref, out_ref, vals_ref, keys_ref, queries_ref):
    sources, _, rows, _ = x_ref.shape
    txt = rows - vid
    row = lax.broadcasted_iota(jnp.int32, (rows, HEAD), 0)
    for s in range(sources):
        valid = (row < vid) | (row - vid + s * txt < length_ref[0])
        here = pl.ds(s * rows, rows)
        queries_ref[here, :] = x_ref[s, 0]
        keys_ref[here, :] = x_ref[s, 1]
        vals_ref[here, :HEAD] = x_ref[s, 2]
        vals_ref[here, HEAD:] = jnp.where(valid, 1.0, 0.0).astype(jnp.bfloat16)

    def score(block):
        return lax.dot_general(
            queries_ref[pl.ds(block * GROUP * rows, GROUP * rows), :],
            keys_ref[...],
            (((1,), (1,)), ((), ())),
            preferred_element_type=jnp.float32,
        )

    blocks = sources // GROUP
    following = score(0)
    for block in range(blocks):
        scores = following
        if block + 1 < blocks:
            following = score(block + 1)
        best = jnp.max(scores, axis=1, keepdims=True) * SLOPE
        weights = jnp.exp2(scores * SLOPE - best).astype(jnp.bfloat16)
        both = jnp.dot(weights, vals_ref[...], preferred_element_type=jnp.float32)
        total = both[:, HEAD:]
        mixed = (both[:, :HEAD] / total).astype(jnp.bfloat16)
        wide = (best + jnp.log2(total)) * LN2
        for g in range(GROUP):
            s = block * GROUP + g
            out_ref[s, :rows] = mixed[g * rows : (g + 1) * rows]
            lse = wide[g * rows : (g + 1) * rows].T[:LSE_ROWS]
            high = lse.astype(jnp.bfloat16).astype(jnp.float32)
            mid = (lse - high).astype(jnp.bfloat16).astype(jnp.float32)
            which = lax.broadcasted_iota(jnp.int32, lse.shape, 0)
            parts = jnp.where(which == 0, high, jnp.where(which == 1, mid, lse - high - mid))
            out_ref[s, rows:] = parts.astype(jnp.bfloat16)


def project_kernel(spot_ref, x_ref, gate_ref, *refs):
    pieces = refs[:8]
    av_ref, at_ref, lv_ref, lt_ref, pv_ref, turned_ref, mixed_ref = refs[8:]
    vid = av_ref.shape[0]
    rows = vid + at_ref.shape[0]
    lses = []
    for h in range(HEADS):
        cols = pl.ds(h * HEAD, HEAD)
        av_ref[:, cols] = x_ref[h, :vid]
        at_ref[:, cols] = x_ref[h, vid:rows]
        turned_ref[cols, :] = x_ref[h, :rows].astype(jnp.float32).T.astype(jnp.bfloat16)
        parts = x_ref[h, rows:].astype(jnp.float32)
        lse = parts[0:1] + parts[1:2] + parts[2:3]
        lv_ref[h] = lse[:, :vid]
        lses.append(lse)
    lses += [lses[0]] * (HEAD - HEADS)
    lt_ref[...] = jnp.concatenate(lses, axis=0).T[vid:, :HEADS]

    zl, zh, x, core = spot_ref[0], spot_ref[1], spot_ref[2], spot_ref[3]
    nz, nx = SIZES["zh"], SIZES["x"]
    near = 2 * zl - 1 + nz
    of_z = (zh, zh + near, zh + nz - near, zh + nz // 2)
    of_x = (x, x + nx - 1, x + 1, x + nx // 2)
    depth = pieces[0].shape[0]
    count = depth // nz
    for i in range(len(pieces)):
        for j in range(nz):
            row = (of_z[j] + nz) % nz * nx + of_x[i % nx] % nx
            row = (row * SIZES["core"] + (core ^ (i // nx))) * count
            source = pl.ds(pl.multiple_of(row, 16), count)
            mixed_ref[pl.ds(i * depth + j * count, count), :] = turned_ref[source, :]
    mixed = mixed_ref[...].astype(jnp.float32).T[:vid].astype(jnp.bfloat16)
    width = 512
    for first in range(0, pv_ref.shape[1], width):
        here = pl.ds(first, width)
        out = jnp.zeros((vid, width), jnp.float32)
        for i, piece in enumerate(pieces):
            out += jnp.dot(
                mixed[:, i * depth : (i + 1) * depth], piece[:, here], preferred_element_type=jnp.float32
            )
        pv_ref[:, here] = (out * gate_ref[:, here]).astype(jnp.bfloat16)


def across(block):
    nz = SIZES["zh"]
    between = []
    for zh in range(nz):
        here, there = nz + zh, (zh + 1) % nz
        between += [(here, there), (there, here)]
    return lax.ppermute(block, ("zl", "zh"), between)


def gathered(w_out, first, second):
    nx = SIZES["x"]
    column = jnp.concatenate([w_out, first, second, across(second)], axis=0)
    up = [(i, (i + 1) % nx) for i in range(nx)]
    down = [(i, (i - 1) % nx) for i in range(nx)]
    left = lax.ppermute(column, "x", up)
    right = lax.ppermute(column, "x", down)
    partner = [(0, 1), (1, 0)]
    other = lax.ppermute(column, "core", partner)
    right, other = lax.optimization_barrier((right, other))
    half = column.shape[0] // 2
    far = [lax.ppermute(left[:half], "x", up), lax.ppermute(right[half:], "x", down)]
    mine = [left, right, jnp.concatenate(far, axis=0)]
    return [column, *mine, other, *(lax.ppermute(part, "core", partner) for part in mine)]


def shards(sources, q_video, kv_video, q_text, kv_text, text_lengths, gate, w_out):
    vid, feats = q_video.shape[1:]
    txt = q_text.shape[1]
    rows = vid + txt
    base = (lax.axis_index(SEQ) * txt).astype(jnp.int32).reshape(1)
    first = across(w_out)
    second = lax.ppermute(first, "zl", [(0, 1), (1, 0)])
    pieces = gathered(w_out, first, second)
    spot = jnp.stack([lax.axis_index(axis) for axis in ("zl", "zh", "x", "core")])
    smem = pl.BlockSpec(memory_space=pltpu.SMEM)
    vmem = pl.BlockSpec(memory_space=VMEM)
    anywhere = pl.BlockSpec(memory_space=pl.ANY)
    packed = pl.pallas_call(
        pack_kernel,
        out_shape=jax.ShapeDtypeStruct((sources, 3, rows, HEAD), jnp.bfloat16),
        in_specs=[smem, smem, anywhere, anywhere, anywhere, anywhere],
        out_specs=vmem,
        scratch_shapes=[
            VMEM((vid, feats), jnp.bfloat16),
            VMEM((vid, 2, feats), jnp.bfloat16),
            VMEM((txt, feats), jnp.bfloat16),
            VMEM((txt, 2, feats), jnp.bfloat16),
            VMEM((HEADS, 2 * rows, HEAD), jnp.float32),
            pltpu.SemaphoreType.DMA((4,)),
        ],
        compiler_params=pltpu.CompilerParams(vmem_limit_bytes=60 << 20),
        name="pack",
    )(
        text_lengths,
        base,
        q_video[0],
        kv_video[0],
        q_text[0],
        kv_text[0],
    )
    packed = lax.optimization_barrier((packed, first))[0]
    moved = lax.all_to_all(packed, SEQ, 0, 0, tiled=True)
    mixed = pl.pallas_call(
        functools.partial(attend_kernel, vid),
        out_shape=jax.ShapeDtypeStruct((sources, rows + LSE_ROWS, HEAD), jnp.bfloat16),
        in_specs=[smem, vmem],
        out_specs=vmem,
        scratch_shapes=[
            VMEM((sources * rows, 2 * HEAD), jnp.bfloat16),
            VMEM((sources * rows, HEAD), jnp.bfloat16),
            VMEM((sources * rows, HEAD), jnp.bfloat16),
        ],
        compiler_params=pltpu.CompilerParams(vmem_limit_bytes=40 << 20),
        name="attend",
    )(text_lengths, moved)
    back = lax.all_to_all(mixed, SEQ, 0, 0, tiled=True)
    attn_video, attn_text, lse_video, lse_text, proj_video = pl.pallas_call(
        project_kernel,
        out_shape=(
            jax.ShapeDtypeStruct((vid, feats), jnp.bfloat16),
            jax.ShapeDtypeStruct((txt, feats), jnp.bfloat16),
            jax.ShapeDtypeStruct((HEADS, 1, vid), jnp.float32),
            jax.ShapeDtypeStruct((txt, HEADS), jnp.float32),
            jax.ShapeDtypeStruct((vid, feats), jnp.bfloat16),
        ),
        in_specs=[smem, *[vmem] * (2 + len(pieces))],
        out_specs=(vmem,) * 5,
        scratch_shapes=[VMEM((feats, rows), jnp.bfloat16)] * 2,
        compiler_params=pltpu.CompilerParams(vmem_limit_bytes=16 << 20),
        name="project",
    )(spot.astype(jnp.int32), back, gate, *pieces)
    return (
        attn_video[None],
        attn_text[None],
        lse_video.transpose(1, 0, 2),
        lse_text.T[None],
        proj_video[None],
    )


def solution(mesh):
    sources = mesh.shape["seq"]
    mesh = Mesh(mesh.devices.reshape(tuple(SIZES.values())), tuple(SIZES))
    placed = (
        P(FSDP, SEQ, None),
        P(FSDP, SEQ, None, None),
        P(FSDP, SEQ, None),
        P(FSDP, SEQ, None, None),
        P(FSDP),
        P(FSDP, None),
        P(FSDP, None),
    )
    return jax.shard_map(
        functools.partial(shards, sources),
        mesh=mesh,
        in_specs=placed,
        out_specs=(
            P(FSDP, SEQ, None),
            P(FSDP, SEQ, None),
            P(FSDP, None, SEQ),
            P(FSDP, None, SEQ),
            P(FSDP, SEQ, None),
        ),
        check_vma=False,
    )
```
